32 devices in a mesh: members: 2 (over y), areal: 8 (over z, x), layer: 2 (over core).
Axes of the slice: x: 2, y: 2, z: 4, core: 2. Of those that a mesh axis runs over, the one named last changes fastest.
Arguments:
- pressure: float32 [32, 64, 512], P(('members', 'layer'), 'areal'), parts along dimension 0, may hold values from -6 to 6
- saturation: float32 [32, 64, 512], P(('members', 'layer'), 'areal'), parts along dimension 0, may hold values from 0.05 to 0.95
- sat_cotangent: float32 [32, 64, 512], P(('members', 'layer'), 'areal'), parts along dimension 0, may hold values from -12 to 12
- dt_over_pv: float32 [32, 64, 512], P(('members', 'layer'), 'areal'), parts along dimension 0, may hold values from 0.3 to 3
- compress: float32 [32, 64, 512], P(('members', 'layer'), 'areal'), parts along dimension 0, may hold values from 0.05 to 0.5
- trans: float32 [3, 32, 64, 512], P(None, ('members', 'layer'), 'areal'), parts along dimension 1, may hold values from 0.2 to 5
- cell_flags: int32 [32, 64, 512], P(('members', 'layer'), 'areal'), parts along dimension 0, may hold values from 0 to 15, as said below
- well_cells: int32 [128], P('members'), parts along dimension 0, may hold values from 0 to 524287
- well_misfit: float32 [128], P('members'), parts along dimension 0, may hold values from -12 to 12
Outputs:
- sat_adjoint: float32 [32, 64, 512], P(('members', 'layer'), 'areal'), parts along dimension 0
- pressure_adjoint: float32 [32, 64, 512], P(('members', 'layer'), 'areal'), parts along dimension 0
The draws below stay inside these ranges and needn't reach their ends.
There are 2 independent parts, one for each index of `members`. The reference program is written for one: setup_inputs(seed, part) draws one part's arguments, and reference() takes and returns one part's arrays. A program takes and returns all parts, laid end to end along the dimension named above; each array names one. Nothing has to cross between parts.
Inputs may be any that keep to these rules, and one draw needn't show every extreme that they name: `cell_flags`: bits 0, 1, 2: the cell is upwind on its upper face along z, x, y; bit 3: the cell is active. `well_cells`: index (z * 64 + x) * 512 + y of the well's cell; wells may share a cell.
All inputs are finite; a program needn't handle non-finite values.
Results may differ from the reference program's by a relative error of at most 0.0001.
Values sent between devices are 32-bit elements; how exact they have to be, the bound alone decides.
A program may use at most 64 MiB of HBM per device.

```python
import math
import jax
import jax.numpy as jnp

CZ = 8
NY = 512
ITERS = 4
NWELL = 64
NZ = 16
NX = 64


def draw_sat_cotangent(key, part):
    key = jax.random.fold_in(key, 11)
    first = jax.random.fold_in(key, 0)
    ramp = jnp.exp(jnp.log(3.0) * jnp.arange(NX, dtype=jnp.float32) / (NX - 1))[None, :, None]
    base = jnp.clip(jax.random.normal(first, (NZ, NX, NY), jnp.float32), -4.0, 4.0)
    return (base * ramp).astype(jnp.float32)


def draw_cell_flags(key, part):
    key = jax.random.fold_in(key, 23)
    first, second = jax.random.split(key)
    upwind = jax.random.randint(first, (NZ, NX, NY), 0, 8)
    active = (jax.random.randint(second, (NZ, NX, NY), 0, 10) > 0).astype(jnp.int32)
    return (upwind + 8 * active).astype(jnp.int32)


def plant(values, rng, low, high):
    shape = values.shape
    spot = [jax.random.randint(jax.random.fold_in(rng, axis), (), 0, shape[axis]) for axis in range(len(shape))]
    values = values.at[tuple(spot)].set(low)
    longest = shape.index(max(shape))
    spot[longest] = (spot[longest] + 1) % shape[longest]
    return values.at[tuple(spot)].set(high)


def steps_of(own_key, dims, cuts, least, largest):
    factor_of = 1.0
    for dim, parts in cuts:
        heights = jax.random.uniform(jax.random.fold_in(jax.random.fold_in(own_key, 6), dim), (parts,), jnp.float32, least / len(cuts), largest / len(cuts))
        factor_of = factor_of * jnp.repeat(jnp.exp(heights), dims[dim] // parts).reshape((-1,) + (1,) * (len(dims) - 1 - dim))
    return factor_of


def centred(stream_key, dims, spread, bound, cuts=(), held_as=jnp.bfloat16):
    values = spread * jax.random.normal(stream_key, dims, jnp.float32)
    if cuts:
        values = values * steps_of(stream_key, dims, cuts, -0.22, 0.18)
    return jnp.clip(values, -bound, bound).astype(held_as)


def setup_inputs(seed: int = 0, part: int = 0) -> dict:
    splits = jax.random.split(jax.random.key(seed), 10)
    part_keys = jax.random.split(jax.random.fold_in(splits[9], part), 10)
    pressure = centred(part_keys[0], (NZ, NX, NY), 1.0, 6.0, ((0, 2), (1, 8)), jnp.float32)
    saturation = jnp.clip(0.05 + 0.9 * jax.random.uniform(part_keys[1], (NZ, NX, NY), jnp.float32) ** steps_of(part_keys[1], (NZ, NX, NY), ((0, 2), (1, 8)), -0.2, 0.2), 0.05, 0.95)
    sat_cotangent = draw_sat_cotangent(jax.random.fold_in(jax.random.fold_in(splits[9], part), 71), part)
    dt_over_pv = jnp.clip(jnp.exp(math.log(3.0) - 2.3025851 * jax.random.uniform(part_keys[3], (NZ, NX, NY), jnp.float32) ** steps_of(part_keys[3], (NZ, NX, NY), ((0, 2), (1, 8)), -0.2, 0.2)), 0.3, 3.0)
    compress = jnp.clip(jnp.exp(math.log(0.5) - 2.3025851 * jax.random.uniform(part_keys[4], (NZ, NX, NY), jnp.float32) ** steps_of(part_keys[4], (NZ, NX, NY), ((0, 2), (1, 8)), -0.2, 0.2)), 0.05, 0.5)
    trans = jnp.clip(jnp.exp(math.log(5.0) - 3.218876 * jax.random.uniform(part_keys[5], (3, NZ, NX, NY), jnp.float32) ** steps_of(part_keys[5], (3, NZ, NX, NY), ((1, 2), (2, 8)), -0.2, 0.2)), 0.2, 5.0)
    cell_flags = draw_cell_flags(jax.random.fold_in(jax.random.fold_in(splits[9], part), 71), part)
    well_cells = plant(jax.random.randint(part_keys[7], (NWELL,), 0, NZ * NX * NY), jax.random.fold_in(part_keys[7], 1), 0, (NZ * NX * NY) - 1).astype(jnp.int32)
    well_misfit = centred(part_keys[8], (NWELL,), 3.0, 12.0, (), jnp.float32)
    return {"pressure": pressure, "saturation": saturation, "sat_cotangent": sat_cotangent, "dt_over_pv": dt_over_pv, "compress": compress, "trans": trans, "cell_flags": cell_flags, "well_cells": well_cells, "well_misfit": well_misfit}


mobility_ratio = 0.5


def flow_fraction(wetness):
    square = wetness * wetness
    other = (1.0 - wetness) * (1.0 - wetness)
    denominator = square + mobility_ratio * other
    return square / denominator, 2.0 * mobility_ratio * wetness * (1.0 - wetness) / (denominator * denominator)


def offset_view(padded, axis_pos, offset):
    bounds = [slice(1, -1), slice(1, -1), slice(1, -1)]
    bounds[axis_pos] = slice(1 + offset, padded.shape[axis_pos] - 1 + offset)
    return padded[tuple(bounds)]


def flag_bit(flags_in, bit_place):
    return jnp.bitwise_and(jnp.right_shift(flags_in, bit_place), 1).astype(jnp.float32)


def transpose_step(pressure_pad, scaled_pad, wetness_pad, active_pad, trans_pads, upwind_pads, modified):
    pushed = jnp.zeros_like(modified)
    driven = jnp.zeros_like(modified)
    upper_terms = []
    lower_terms = []
    for axis_pos in range(3):
        upper_face = offset_view(trans_pads[axis_pos], axis_pos, 0) * offset_view(active_pad, axis_pos, 1)
        lower_face = offset_view(trans_pads[axis_pos], axis_pos, -1) * offset_view(active_pad, axis_pos, 0)
        flag_upper = offset_view(upwind_pads[axis_pos], axis_pos, 0)
        flag_lower = offset_view(upwind_pads[axis_pos], axis_pos, -1)
        wet_here = offset_view(wetness_pad, axis_pos, 0)
        wet_upper = flag_upper * wet_here + (1.0 - flag_upper) * offset_view(wetness_pad, axis_pos, 1)
        wet_lower = flag_lower * offset_view(wetness_pad, axis_pos, -1) + (1.0 - flag_lower) * wet_here
        frac_upper, slope_upper = flow_fraction(wet_upper)
        frac_lower, slope_lower = flow_fraction(wet_lower)
        scaled_here = offset_view(scaled_pad, axis_pos, 0)
        jump_upper = offset_view(scaled_pad, axis_pos, 1) - scaled_here
        jump_lower = scaled_here - offset_view(scaled_pad, axis_pos, -1)
        press_here = offset_view(pressure_pad, axis_pos, 0)
        flux_upper = upper_face * (press_here - offset_view(pressure_pad, axis_pos, 1))
        flux_lower = lower_face * (offset_view(pressure_pad, axis_pos, -1) - press_here)
        pushed = pushed + upper_face * jump_upper * frac_upper - lower_face * jump_lower * frac_lower
        driven = driven + flag_upper * jump_upper * flux_upper * slope_upper + (1.0 - flag_lower) * jump_lower * flux_lower * slope_lower
        upper_terms.append(upper_face)
        lower_terms.append(lower_face)
    return pushed, modified + driven, upper_terms, lower_terms


def apply_operator(vector_pad, compress, upper_terms, lower_terms):
    center = offset_view(vector_pad, 0, 0)
    result = compress * center
    for axis_pos in range(3):
        result = result + upper_terms[axis_pos] * (center - offset_view(vector_pad, axis_pos, 1)) + lower_terms[axis_pos] * (center - offset_view(vector_pad, axis_pos, -1))
    return result


def layer_solve(diagonal, coupling, source, depth):
    shape_full = source.shape
    blocks = (-1, depth) + tuple(shape_full[1:])
    diagonal = diagonal.reshape(blocks)
    coupling = coupling.reshape(blocks)
    source = source.reshape(blocks)
    ratios = [-coupling[:, 0] / diagonal[:, 0]]
    partial_sol = [source[:, 0] / diagonal[:, 0]]
    for level in range(1, depth):
        pivot = diagonal[:, level] + coupling[:, level - 1] * ratios[level - 1]
        ratios.append(-coupling[:, level] / pivot)
        partial_sol.append((source[:, level] + coupling[:, level - 1] * partial_sol[level - 1]) / pivot)
    solved = [partial_sol[depth - 1]]
    for level in range(depth - 2, -1, -1):
        solved.insert(0, partial_sol[level] - ratios[level] * solved[0])
    return jnp.stack(solved, axis=1).reshape(shape_full)


def reference(pressure, saturation, sat_cotangent, dt_over_pv, compress, trans, cell_flags, well_cells, well_misfit):
    modified = sat_cotangent.reshape(-1).at[well_cells].add(well_misfit).reshape(sat_cotangent.shape)
    scaled = dt_over_pv * modified
    bits = [flag_bit(cell_flags, bit_place) for bit_place in range(4)]
    active = bits[3]
    trans_live = trans * active[None]
    trans_pads = tuple(jnp.pad(trans_live[axis_pos], 1) for axis_pos in range(3))
    upwind_pads = tuple(jnp.pad(bits[axis_pos], 1) for axis_pos in range(3))
    pushed, sat_adjoint, upper_terms, lower_terms = transpose_step(jnp.pad(pressure, 1), jnp.pad(scaled, 1), jnp.pad(saturation, 1), jnp.pad(active, 1), trans_pads, upwind_pads, modified)
    diagonal = compress
    for axis_pos in range(3):
        diagonal = diagonal + upper_terms[axis_pos] + lower_terms[axis_pos]
    solution = jnp.zeros_like(pushed)
    resid = pushed
    smoothed = layer_solve(diagonal, upper_terms[0], resid, CZ)
    search = smoothed
    gamma = jnp.sum(resid * smoothed)
    for step in range(ITERS):
        image = apply_operator(jnp.pad(search, 1), compress, upper_terms, lower_terms)
        alpha = gamma / jnp.sum(search * image)
        solution = solution + alpha * search
        resid = resid - alpha * image
        if step + 1 < ITERS:
            smoothed = layer_solve(diagonal, upper_terms[0], resid, CZ)
            gamma_next = jnp.sum(resid * smoothed)
            search = smoothed + (gamma_next / gamma) * search
            gamma = gamma_next
    return sat_adjoint, solution
```

```python
import functools

import jax
import jax.numpy as jnp
from jax import lax
from jax.experimental import pallas as pl
from jax.experimental.pallas import tpu as pltpu
from jax.sharding import PartitionSpec as P

ITERS = 4
MOBILITY_RATIO = 0.5
LOW_GROUP = 8
MESH = pl.DeviceIdType.MESH


def flow_fraction(wetness):
    square = wetness * wetness
    dry = 1.0 - wetness
    inverse = 1.0 / (square + MOBILITY_RATIO * (dry * dry))
    return square * inverse, (2.0 * MOBILITY_RATIO) * wetness * dry * (inverse * inverse)


def face_terms(face, scaled, press, frac, slope, upwind):
    moved = face * (scaled[1] - scaled[0])
    push = moved * jnp.where(upwind, frac[0], frac[1])
    drive = moved * (press[0] - press[1]) * jnp.where(upwind, slope[0], slope[1])
    return push, jnp.where(upwind, drive, 0.0), jnp.where(upwind, 0.0, drive)


def galerkin(moments):
    def inner(i, j):
        return 0.5 * (moments[i + j] + moments[abs(i - j)])

    def entry(i, j):
        moved = inner(i, 1) if j == 0 else 0.5 * (inner(i, j + 1) + inner(i, j - 1))
        return inner(i, j) - moved

    size = ITERS
    lower = [[None] * size for _ in range(size)]
    inverse = []
    forward = []
    for i in range(size):
        for j in range(i):
            total = entry(i, j)
            for k in range(j):
                total = total - lower[i][k] * lower[j][k] * inverse[k]
            lower[i][j] = total
        diagonal = entry(i, i)
        pivot = diagonal
        right = moments[i]
        for k in range(i):
            scale = lower[i][k] * inverse[k]
            pivot = pivot - scale * lower[i][k]
            right = right - scale * forward[k]
        keep = pivot > 1e-6 * diagonal
        inv = jnp.where(keep, 1.0 / jnp.where(keep, pivot, 1.0), 0.0)
        inverse.append(inv)
        forward.append(right)
    solved = [None] * size
    for i in range(size - 1, -1, -1):
        total = forward[i]
        for k in range(i + 1, size):
            total = total - lower[k][i] * solved[k]
        solved[i] = total * inverse[i]
    return solved


def kernel(
    areal_count,
    press_in, wet_in, cot_in, dt_in, comp_in, trans_in, flags_in, cells_in, misfit_in,
    sat_out, sol_out,
    press, wet, cot, dt, comp, trans, flags, cells, misfit,
    scaled, frac, slope, resid, sat_res, sol_res,
    face_z, inv_pivot, down_gain, up_gain,
    face_xu, face_xl, face_yu, face_yl, face_edge, face_zedge,
    basis, source,
    send_hi, send_lo, send_z, recv_hi, recv_lo, recv_z,
    vec_hi, vec_lo, got_hi, got_lo, got_z,
    sums, others,
    in_sem, out_sem, face_send, face_recv, vec_send, vec_recv, sum_send, sum_recv,
):
    depth, width, span = press.shape
    areal = lax.axis_index("areal")
    layer = lax.axis_index("layer")
    has_lo = areal > 0
    has_hi = areal < areal_count - 1
    lower_id = {"areal": jnp.maximum(areal - 1, 0), "layer": layer}
    upper_id = {"areal": jnp.minimum(areal + 1, areal_count - 1), "layer": layer}
    other_id = {"areal": areal, "layer": 1 - layer}
    edge = (depth - 1) * (1 - layer)

    low = min(LOW_GROUP, areal_count)
    high = areal_count // low
    place = lax.rem(areal, low)
    first = areal - place
    flat = place * 2 + layer
    stages = [[]]
    for step in range(1, 2 * low):
        peer = lax.rem(flat + step, 2 * low)
        stages[0].append({"areal": first + lax.div(peer, 2), "layer": lax.rem(peer, 2)})
    if high > 1:
        row = lax.div(areal, low)
        stages.append(
            [
                {"areal": lax.rem(row + step, high) * low + place, "layer": layer}
                for step in range(1, high)
            ]
        )

    pairs = [
        (cells_in, cells), (misfit_in, misfit), (cot_in, cot), (dt_in, dt), (flags_in, flags),
        (press_in, press), (wet_in, wet), (trans_in, trans), (comp_in, comp),
    ]
    loads = [
        pltpu.make_async_copy(src, dst, in_sem.at[place_of])
        for place_of, (src, dst) in enumerate(pairs)
    ]
    for load in loads:
        load.start()

    barrier = pltpu.get_barrier_semaphore()
    for stage in stages:
        for peer_id in stage:
            pl.semaphore_signal(barrier, inc=1, device_id=peer_id, device_id_type=MESH)
    expected = sum(len(stage) for stage in stages)
    if high > 1:
        @pl.when(has_lo)
        def _():
            pl.semaphore_signal(barrier, inc=1, device_id=lower_id, device_id_type=MESH)

        @pl.when(has_hi)
        def _():
            pl.semaphore_signal(barrier, inc=1, device_id=upper_id, device_id_type=MESH)

    @pl.when(jnp.logical_not(has_lo))
    def _():
        recv_lo[...] = jnp.zeros_like(recv_lo)
        got_lo[...] = jnp.zeros_like(got_lo)

    @pl.when(jnp.logical_not(has_hi))
    def _():
        recv_hi[...] = jnp.zeros_like(recv_hi)
        got_hi[...] = jnp.zeros_like(got_hi)

    rows = lax.broadcasted_iota(jnp.int32, (width, span), 0)
    lanes = lax.broadcasted_iota(jnp.int32, (width, span), 1)
    is_low_row = rows == 0
    is_high_row = rows == width - 1
    is_last_lane = lanes == span - 1

    def next_y(value):
        return pltpu.roll(value, span - 1, 1)

    def prev_y(value):
        return pltpu.roll(value, 1, 1)

    def next_x(value):
        return pltpu.roll(value, width - 1, 0)

    def prev_x(value):
        return pltpu.roll(value, 1, 0)

    loads[0].wait()
    loads[1].wait()
    cell = cells[...]
    wells = cell.shape[1]
    local = lax.broadcasted_iota(jnp.int32, (depth * width, wells), 0)
    base = (
        (layer * depth + lax.shift_right_logical(local, (width - 1).bit_length()))
        * (areal_count * width)
        + areal * width + lax.bitwise_and(local, width - 1)
    ) * span
    offset = cell - base
    by_row = jnp.where((offset >= 0) & (offset < span), misfit[...], 0.0)
    lane_of = lax.bitwise_and(cell, span - 1)
    by_lane = jnp.where(
        lax.broadcasted_iota(jnp.int32, (span, wells), 0) == lane_of, 1.0, 0.0
    )
    added = lax.dot_general(
        by_row, by_lane, (((1,), (1,)), ((), ())),
        precision=lax.Precision.HIGHEST, preferred_element_type=jnp.float32,
    )
    for load in loads[2:8]:
        load.wait()
    act = []
    for l in range(depth):
        modified = cot[l] + added[l * width : (l + 1) * width]
        sat_res[l] = modified
        scaled[l] = dt[l] * modified
        act.append(jnp.where((flags[l] & 8) != 0, 1.0, 0.0))

    for l in range(depth):
        here = slice(l, l + 1)
        top = slice(width - 1, width)
        live_x = trans[1, l] * act[l]
        up_x = jnp.where((flags[l] & 2) != 0, 1.0, 0.0)
        for k, plane in enumerate((press[l], scaled[l], wet[l], live_x, up_x)):
            send_hi[k, here] = plane[top]
        for k, plane in enumerate((press[l], scaled[l], wet[l], act[l])):
            send_lo[k, here] = plane[0:1]
    edge_act = jnp.where((flags[edge] & 8) != 0, 1.0, 0.0)
    send_z[0] = press[edge]
    send_z[1] = scaled[edge]
    send_z[2] = wet[edge]
    send_z[3] = edge_act
    send_z[4] = trans[0, edge] * edge_act
    send_z[5] = jnp.where((flags[edge] & 1) != 0, 1.0, 0.0)

    pl.semaphore_wait(barrier, expected)
    if high > 1:
        @pl.when(has_lo)
        def _():
            pl.semaphore_wait(barrier, 1)

        @pl.when(has_hi)
        def _():
            pl.semaphore_wait(barrier, 1)

    def remote(src, dst, send_sem, recv_sem, target):
        return pltpu.make_async_remote_copy(
            src_ref=src, dst_ref=dst, send_sem=send_sem, recv_sem=recv_sem,
            device_id=target, device_id_type=MESH,
        )

    def exchange(up_copy, low_copy, z_copy):
        z_copy.start()

        @pl.when(has_hi)
        def _():
            up_copy.start()

        @pl.when(has_lo)
        def _():
            low_copy.start()

    def arrived(up_copy, low_copy, z_copy):
        z_copy.wait_recv()

        @pl.when(has_lo)
        def _():
            up_copy.wait_recv()

        @pl.when(has_hi)
        def _():
            low_copy.wait_recv()

    def departed(up_copy, low_copy, z_copy):
        z_copy.wait_send()

        @pl.when(has_hi)
        def _():
            up_copy.wait_send()

        @pl.when(has_lo)
        def _():
            low_copy.wait_send()

    copies = [
        (
            remote(send_hi, recv_lo, face_send.at[0], face_recv.at[0], upper_id),
            remote(send_lo, recv_hi, face_send.at[1], face_recv.at[1], lower_id),
            remote(send_z, recv_z, face_send.at[2], face_recv.at[2], other_id),
        )
    ]
    exchange(*copies[0])

    for l in range(depth):
        share, rise = flow_fraction(wet[l])
        frac[l] = share
        slope[l] = rise
    carried = None
    for l in range(depth):
        up = (flags[l] & 4) != 0
        face = jnp.where(is_last_lane, 0.0, trans[2, l] * act[l] * next_y(act[l]))
        face_yu[l] = face
        face_yl[l] = prev_y(face)
        push, drive_here, drive_next = face_terms(
            face,
            (scaled[l], next_y(scaled[l])),
            (press[l], next_y(press[l])),
            (frac[l], next_y(frac[l])),
            (slope[l], next_y(slope[l])),
            up,
        )
        pushed = push - prev_y(push)
        driven = sat_res[l] + drive_here + prev_y(drive_next)
        if carried is not None:
            pushed = pushed - carried[0]
            driven = driven + carried[1]
        if l < depth - 1:
            face = trans[0, l] * act[l] * act[l + 1]
            face_z[l] = face
            push, drive_here, drive_next = face_terms(
                face,
                (scaled[l], scaled[l + 1]),
                (press[l], press[l + 1]),
                (frac[l], frac[l + 1]),
                (slope[l], slope[l + 1]),
                (flags[l] & 1) != 0,
            )
            pushed = pushed + push
            driven = driven + drive_here
            carried = (push, drive_next)
        resid[l] = pushed
        sat_res[l] = driven

    arrived(*copies[0])

    below = layer == 0
    z_share, z_rise = flow_fraction(recv_z[2])
    live = jnp.where(below, trans[0, edge] * edge_act * recv_z[3], recv_z[4] * edge_act)
    face_zedge[...] = live
    up_edge = jnp.where(below, send_z[5], recv_z[5]) > 0.5

    def ordered(mine, theirs):
        return jnp.where(below, mine, theirs), jnp.where(below, theirs, mine)

    push, drive_here, drive_next = face_terms(
        live,
        ordered(send_z[1], recv_z[1]),
        ordered(send_z[0], recv_z[0]),
        ordered(frac[edge], z_share),
        ordered(slope[edge], z_rise),
        up_edge,
    )
    resid[edge] = resid[edge] + jnp.where(below, push, -push)
    sat_res[edge] = sat_res[edge] + jnp.where(below, drive_here, drive_next)

    hi_share, hi_rise = flow_fraction(recv_hi[2])
    lo_share, lo_rise = flow_fraction(recv_lo[2])
    own_share, own_rise = flow_fraction(send_lo[2])
    low_face = recv_lo[3] * send_lo[3]
    low_push, _, low_drive = face_terms(
        low_face,
        (recv_lo[1], send_lo[1]),
        (recv_lo[0], send_lo[0]),
        (lo_share, own_share),
        (lo_rise, own_rise),
        recv_lo[4] > 0.5,
    )
    hi_press, hi_scaled, hi_act = recv_hi[0], recv_hi[1], recv_hi[3]

    def with_high(value, plane, l):
        return jnp.where(is_high_row, plane[l : l + 1], next_x(value))

    def with_low(value, plane, l):
        return jnp.where(is_low_row, plane[l : l + 1], prev_x(value))

    loads[8].wait()
    for l in range(depth):
        face = trans[1, l] * act[l] * with_high(act[l], hi_act, l)
        push, drive_here, drive_next = face_terms(
            face,
            (scaled[l], with_high(scaled[l], hi_scaled, l)),
            (press[l], with_high(press[l], hi_press, l)),
            (frac[l], with_high(frac[l], hi_share, l)),
            (slope[l], with_high(slope[l], hi_rise, l)),
            (flags[l] & 2) != 0,
        )
        resid[l] = resid[l] + push - with_low(push, low_push, l)
        sat_res[l] = sat_res[l] + drive_here + with_low(drive_next, low_drive, l)
        face_low = with_low(face, low_face, l)
        face_xu[l] = jnp.where(is_high_row, 0.0, face)
        face_xl[l] = jnp.where(is_low_row, 0.0, face_low)
        face_edge[l] = jnp.where(
            is_high_row, face, jnp.where(is_low_row, face_low, 0.0)
        )
        diagonal = comp[l] + face + face_low + face_yu[l] + face_yl[l]
        if l > 0:
            diagonal = diagonal + face_z[l - 1]
        else:
            diagonal = diagonal + jnp.where(below, 0.0, live)
        if l < depth - 1:
            diagonal = diagonal + face_z[l]
        else:
            diagonal = diagonal + jnp.where(below, live, 0.0)
        pivot = diagonal if l == 0 else diagonal - face_z[l - 1] * up_gain[l - 1]
        inverse = 1.0 / pivot
        inv_pivot[l] = inverse
        if l > 0:
            down_gain[l] = face_z[l - 1] * inverse
        if l < depth - 1:
            up_gain[l] = face_z[l] * inverse

    store_sat = pltpu.make_async_copy(sat_res, sat_out, out_sem.at[0])
    store_sat.start()

    def moment(left, right):
        total = None
        for l in range(depth):
            term = left[l] * right[l]
            total = term if total is None else total + term
        return total

    def fold(plane):
        total = plane[:, 0:128]
        for start in range(128, span, 128):
            total = total + plane[:, start : start + 128]
        return jnp.sum(total, axis=0, keepdims=True)

    older = None
    current = [resid[l] for l in range(depth)]
    products = []
    for step in range(ITERS):
        partial = [current[0] * inv_pivot[0]]
        for l in range(1, depth):
            partial.append(current[l] * inv_pivot[l] + down_gain[l] * partial[l - 1])
        vector = [None] * depth
        vector[depth - 1] = partial[depth - 1]
        for l in range(depth - 2, -1, -1):
            vector[l] = partial[l] + up_gain[l] * vector[l + 1]
        for l in range(depth):
            basis[step, l] = vector[l]
            vec_hi[step, l : l + 1] = vector[l][width - 1 : width]
            vec_lo[step, l : l + 1] = vector[l][0:1]
        tags = [3 * step + k for k in range(3)]
        trio = (
            remote(
                vec_hi.at[step], got_lo.at[step],
                vec_send.at[tags[0]], vec_recv.at[tags[0]], upper_id,
            ),
            remote(
                vec_lo.at[step], got_hi.at[step],
                vec_send.at[tags[1]], vec_recv.at[tags[1]], lower_id,
            ),
            remote(
                basis.at[step, edge], got_z.at[step],
                vec_send.at[tags[2]], vec_recv.at[tags[2]], other_id,
            ),
        )
        copies.append(trio)
        exchange(*trio)
        products.append(fold(moment(vector, current)))
        for l in range(depth):
            near = (
                face_xu[l] * next_x(vector[l])
                + face_xl[l] * prev_x(vector[l])
                + face_yu[l] * next_y(vector[l])
                + face_yl[l] * prev_y(vector[l])
            )
            source[l] = near
        arrived(*trio)
        source[edge] = source[edge] + face_zedge[...] * got_z[step]
        later = []
        for l in range(depth):
            halo = jnp.where(
                rows < width // 2, got_lo[step, l : l + 1], got_hi[step, l : l + 1]
            )
            value = source[l] + face_edge[l] * halo
            if step > 0:
                value = 2.0 * value - older[l]
            later.append(value)
        products.append(fold(moment(vector, later)))
        older, current = current, later

    for k, value in enumerate(products):
        sums[0, k : k + 1] = value
    sends = []
    slot = 0
    for place_of, stage in enumerate(stages):
        batch = [
            remote(
                sums.at[place_of], others.at[slot + k],
                sum_send.at[slot + k], sum_recv.at[slot + k], peer_id,
            )
            for k, peer_id in enumerate(stage)
        ]
        for copy in batch:
            copy.start()
        total = sums[place_of]
        for k, copy in enumerate(batch):
            copy.wait_recv()
        for k in range(len(batch)):
            total = total + others[slot + k]
        if place_of + 1 < len(stages):
            sums[place_of + 1] = total
        sends += batch
        slot += len(batch)
    total = jnp.sum(total, axis=1, keepdims=True)
    raw = [total[k : k + 1] for k in range(2 * ITERS)]
    moments = [raw[0], raw[1]]
    for k in range(2, 2 * ITERS):
        moments.append(2.0 * raw[k] - raw[k % 2])
    weights = [jnp.broadcast_to(value, (width, span)) for value in galerkin(moments)]
    for l in range(depth):
        value = weights[0] * basis[0, l]
        for step in range(1, ITERS):
            value = value + weights[step] * basis[step, l]
        sol_res[l] = value
    store_sol = pltpu.make_async_copy(sol_res, sol_out, out_sem.at[1])
    store_sol.start()
    for trio in copies:
        departed(*trio)
    for copy in sends:
        copy.wait_send()
    store_sat.wait()
    store_sol.wait()


def on_device(areal_count, *arrays):
    arrays = list(arrays)
    block = arrays[0].shape
    depth, width, span = block
    wells = arrays[7].shape[0]
    arrays[7] = arrays[7].reshape(1, wells)
    arrays[8] = arrays[8].reshape(1, wells)
    plane = (width, span)
    strip = (depth, span)
    low = min(LOW_GROUP, areal_count)
    slots = 2 * low - 1 + (areal_count // low - 1)
    f32 = jnp.float32
    cube = pltpu.VMEM(block, f32)

    def vmem(*shape):
        return pltpu.VMEM(shape, f32)

    scratch = [
        cube, cube, cube, cube, cube, vmem(3, *block), pltpu.VMEM(block, jnp.int32),
        pltpu.VMEM((1, wells), jnp.int32), vmem(1, wells),
        cube, cube, cube, cube, cube, cube,
        cube, cube, cube, cube,
        cube, cube, cube, cube, cube, vmem(*plane),
        vmem(ITERS, *block), cube,
        vmem(5, *strip), vmem(4, *strip), vmem(6, *plane),
        vmem(4, *strip), vmem(5, *strip), vmem(6, *plane),
        vmem(ITERS, *strip), vmem(ITERS, *strip),
        vmem(ITERS, *strip), vmem(ITERS, *strip), vmem(ITERS, *plane),
        vmem(2, 2 * ITERS, 128), vmem(slots, 2 * ITERS, 128),
        pltpu.SemaphoreType.DMA((9,)), pltpu.SemaphoreType.DMA((2,)),
        pltpu.SemaphoreType.DMA((3,)), pltpu.SemaphoreType.DMA((3,)),
        pltpu.SemaphoreType.DMA((3 * ITERS,)), pltpu.SemaphoreType.DMA((3 * ITERS,)),
        pltpu.SemaphoreType.DMA((slots,)), pltpu.SemaphoreType.DMA((slots,)),
    ]
    return pl.pallas_call(
        functools.partial(kernel, areal_count),
        out_shape=(jax.ShapeDtypeStruct(block, f32), jax.ShapeDtypeStruct(block, f32)),
        in_specs=[pl.BlockSpec(memory_space=pl.ANY)] * len(arrays),
        out_specs=(pl.BlockSpec(memory_space=pl.ANY), pl.BlockSpec(memory_space=pl.ANY)),
        scratch_shapes=scratch,
        compiler_params=pltpu.CompilerParams(
            collective_id=0, has_side_effects=True, vmem_limit_bytes=32 * 1024 * 1024
        ),
    )(*arrays)


def solution(mesh):
    block = P(("members", "layer"), "areal", None)
    return jax.shard_map(
        functools.partial(on_device, mesh.shape["areal"]),
        mesh=mesh,
        in_specs=(
            block, block, block, block, block,
            P(None, ("members", "layer"), "areal", None),
            block, P("members"), P("members"),
        ),
        out_specs=(block, block),
        check_vma=False,
    )
```

```python
import functools

import jax
import jax.numpy as jnp
from jax import lax
from jax.experimental import pallas as pl
from jax.experimental.pallas import tpu as pltpu
from jax.sharding import PartitionSpec as P

ITERS = 4
MOBILITY_RATIO = 0.5
LOW_GROUP = 8
MESH = pl.DeviceIdType.MESH


def flow_fraction(wetness):
    square = wetness * wetness
    dry = 1.0 - wetness
    inverse = 1.0 / (square + MOBILITY_RATIO * (dry * dry))
    return square * inverse, (2.0 * MOBILITY_RATIO) * wetness * dry * (inverse * inverse)


def face_terms(face, scaled, press, frac, slope, upwind):
    moved = face * (scaled[1] - scaled[0])
    push = moved * jnp.where(upwind, frac[0], frac[1])
    drive = moved * (press[0] - press[1]) * jnp.where(upwind, slope[0], slope[1])
    return push, jnp.where(upwind, drive, 0.0), jnp.where(upwind, 0.0, drive)


def galerkin(moments):
    def inner(i, j):
        return 0.5 * (moments[i + j] + moments[abs(i - j)])

    def entry(i, j):
        moved = inner(i, 1) if j == 0 else 0.5 * (inner(i, j + 1) + inner(i, j - 1))
        return inner(i, j) - moved

    size = ITERS
    lower = [[None] * size for _ in range(size)]
    inverse = []
    forward = []
    for i in range(size):
        for j in range(i):
            total = entry(i, j)
            for k in range(j):
                total = total - lower[i][k] * lower[j][k] * inverse[k]
            lower[i][j] = total
        diagonal = entry(i, i)
        pivot = diagonal
        right = moments[i]
        for k in range(i):
            scale = lower[i][k] * inverse[k]
            pivot = pivot - scale * lower[i][k]
            right = right - scale * forward[k]
        keep = pivot > 1e-6 * diagonal
        inv = jnp.where(keep, 1.0 / jnp.where(keep, pivot, 1.0), 0.0)
        inverse.append(inv)
        forward.append(right)
    solved = [None] * size
    for i in range(size - 1, -1, -1):
        total = forward[i]
        for k in range(i + 1, size):
            total = total - lower[k][i] * solved[k]
        solved[i] = total * inverse[i]
    return solved


def kernel(
    areal_count,
    press_in, wet_in, cot_in, dt_in, comp_in, trans_in, flags_in, cells_in, misfit_in,
    sat_out, sol_out,
    press, wet, cot, dt, comp, trans, flags, cells, misfit,
    scaled, frac, slope, resid, sat_res, sol_res,
    face_z, inv_pivot, down_gain, up_gain,
    face_xu, face_xl, face_yu, face_yl, face_edge, face_zedge,
    basis, source,
    send_hi, send_lo, send_z, recv_hi, recv_lo, recv_z,
    vec_hi, vec_lo, got_hi, got_lo, got_z,
    sums, others,
    in_sem, out_sem, face_send, face_recv, vec_send, vec_recv, sum_send, sum_recv,
):
    depth, width, span = press.shape
    areal = lax.axis_index("areal")
    layer = lax.axis_index("layer")
    has_lo = areal > 0
    has_hi = areal < areal_count - 1
    lower_id = {"areal": jnp.maximum(areal - 1, 0), "layer": layer}
    upper_id = {"areal": jnp.minimum(areal + 1, areal_count - 1), "layer": layer}
    other_id = {"areal": areal, "layer": 1 - layer}
    edge = (depth - 1) * (1 - layer)

    low = min(LOW_GROUP, areal_count)
    high = areal_count // low
    place = lax.rem(areal, low)
    first = areal - place
    stages = [
        [other_id],
        [
            {"areal": first + lax.rem(place + step, low), "layer": layer}
            for step in range(1, low)
        ],
    ]
    if high > 1:
        row = lax.div(areal, low)
        stages.append(
            [
                {"areal": lax.rem(row + step, high) * low + place, "layer": layer}
                for step in range(1, high)
            ]
        )

    pairs = [
        (cells_in, cells), (misfit_in, misfit), (cot_in, cot), (dt_in, dt), (flags_in, flags),
        (press_in, press), (wet_in, wet), (trans_in, trans), (comp_in, comp),
    ]
    loads = [
        pltpu.make_async_copy(src, dst, in_sem.at[place_of])
        for place_of, (src, dst) in enumerate(pairs)
    ]
    for load in loads:
        load.start()

    barrier = pltpu.get_barrier_semaphore()
    for stage in stages:
        for peer_id in stage:
            pl.semaphore_signal(barrier, inc=1, device_id=peer_id, device_id_type=MESH)
    expected = sum(len(stage) for stage in stages)
    if high > 1:
        @pl.when(has_lo)
        def _():
            pl.semaphore_signal(barrier, inc=1, device_id=lower_id, device_id_type=MESH)

        @pl.when(has_hi)
        def _():
            pl.semaphore_signal(barrier, inc=1, device_id=upper_id, device_id_type=MESH)

    @pl.when(jnp.logical_not(has_lo))
    def _():
        recv_lo[...] = jnp.zeros_like(recv_lo)
        got_lo[...] = jnp.zeros_like(got_lo)

    @pl.when(jnp.logical_not(has_hi))
    def _():
        recv_hi[...] = jnp.zeros_like(recv_hi)
        got_hi[...] = jnp.zeros_like(got_hi)

    rows = lax.broadcasted_iota(jnp.int32, (width, span), 0)
    lanes = lax.broadcasted_iota(jnp.int32, (width, span), 1)
    is_low_row = rows == 0
    is_high_row = rows == width - 1
    is_last_lane = lanes == span - 1

    def next_y(value):
        return pltpu.roll(value, span - 1, 1)

    def prev_y(value):
        return pltpu.roll(value, 1, 1)

    def next_x(value):
        return pltpu.roll(value, width - 1, 0)

    def prev_x(value):
        return pltpu.roll(value, 1, 0)

    loads[0].wait()
    loads[1].wait()
    cell = cells[...]
    wells = cell.shape[1]
    local = lax.broadcasted_iota(jnp.int32, (depth * width, wells), 0)
    base = (
        (layer * depth + lax.shift_right_logical(local, (width - 1).bit_length()))
        * (areal_count * width)
        + areal * width + lax.bitwise_and(local, width - 1)
    ) * span
    offset = cell - base
    by_row = jnp.where((offset >= 0) & (offset < span), misfit[...], 0.0)
    lane_of = lax.bitwise_and(cell, span - 1)
    by_lane = jnp.where(
        lax.broadcasted_iota(jnp.int32, (span, wells), 0) == lane_of, 1.0, 0.0
    )
    added = lax.dot_general(
        by_row, by_lane, (((1,), (1,)), ((), ())),
        precision=lax.Precision.HIGHEST, preferred_element_type=jnp.float32,
    )
    for load in loads[2:8]:
        load.wait()
    act = []
    for l in range(depth):
        modified = cot[l] + added[l * width : (l + 1) * width]
        sat_res[l] = modified
        scaled[l] = dt[l] * modified
        act.append(jnp.where((flags[l] & 8) != 0, 1.0, 0.0))

    for l in range(depth):
        here = slice(l, l + 1)
        top = slice(width - 1, width)
        live_x = trans[1, l] * act[l]
        up_x = jnp.where((flags[l] & 2) != 0, 1.0, 0.0)
        for k, plane in enumerate((press[l], scaled[l], wet[l], live_x, up_x)):
            send_hi[k, here] = plane[top]
        for k, plane in enumerate((press[l], scaled[l], wet[l], act[l])):
            send_lo[k, here] = plane[0:1]
    edge_act = jnp.where((flags[edge] & 8) != 0, 1.0, 0.0)
    send_z[0] = press[edge]
    send_z[1] = scaled[edge]
    send_z[2] = wet[edge]
    send_z[3] = edge_act
    send_z[4] = trans[0, edge] * edge_act
    send_z[5] = jnp.where((flags[edge] & 1) != 0, 1.0, 0.0)

    pl.semaphore_wait(barrier, expected)
    if high > 1:
        @pl.when(has_lo)
        def _():
            pl.semaphore_wait(barrier, 1)

        @pl.when(has_hi)
        def _():
            pl.semaphore_wait(barrier, 1)

    def remote(src, dst, send_sem, recv_sem, target):
        return pltpu.make_async_remote_copy(
            src_ref=src, dst_ref=dst, send_sem=send_sem, recv_sem=recv_sem,
            device_id=target, device_id_type=MESH,
        )

    def exchange(up_copy, low_copy, z_copy):
        z_copy.start()

        @pl.when(has_hi)
        def _():
            up_copy.start()

        @pl.when(has_lo)
        def _():
            low_copy.start()

    def arrived(up_copy, low_copy, z_copy):
        z_copy.wait_recv()

        @pl.when(has_lo)
        def _():
            up_copy.wait_recv()

        @pl.when(has_hi)
        def _():
            low_copy.wait_recv()

    def departed(up_copy, low_copy, z_copy):
        z_copy.wait_send()

        @pl.when(has_hi)
        def _():
            up_copy.wait_send()

        @pl.when(has_lo)
        def _():
            low_copy.wait_send()

    copies = [
        (
            remote(send_hi, recv_lo, face_send.at[0], face_recv.at[0], upper_id),
            remote(send_lo, recv_hi, face_send.at[1], face_recv.at[1], lower_id),
            remote(send_z, recv_z, face_send.at[2], face_recv.at[2], other_id),
        )
    ]
    exchange(*copies[0])

    for l in range(depth):
        share, rise = flow_fraction(wet[l])
        frac[l] = share
        slope[l] = rise
    carried = None
    for l in range(depth):
        up = (flags[l] & 4) != 0
        face = jnp.where(is_last_lane, 0.0, trans[2, l] * act[l] * next_y(act[l]))
        face_yu[l] = face
        face_yl[l] = prev_y(face)
        push, drive_here, drive_next = face_terms(
            face,
            (scaled[l], next_y(scaled[l])),
            (press[l], next_y(press[l])),
            (frac[l], next_y(frac[l])),
            (slope[l], next_y(slope[l])),
            up,
        )
        pushed = push - prev_y(push)
        driven = sat_res[l] + drive_here + prev_y(drive_next)
        if carried is not None:
            pushed = pushed - carried[0]
            driven = driven + carried[1]
        if l < depth - 1:
            face = trans[0, l] * act[l] * act[l + 1]
            face_z[l] = face
            push, drive_here, drive_next = face_terms(
                face,
                (scaled[l], scaled[l + 1]),
                (press[l], press[l + 1]),
                (frac[l], frac[l + 1]),
                (slope[l], slope[l + 1]),
                (flags[l] & 1) != 0,
            )
            pushed = pushed + push
            driven = driven + drive_here
            carried = (push, drive_next)
        resid[l] = pushed
        sat_res[l] = driven

    arrived(*copies[0])

    below = layer == 0
    z_share, z_rise = flow_fraction(recv_z[2])
    live = jnp.where(below, trans[0, edge] * edge_act * recv_z[3], recv_z[4] * edge_act)
    face_zedge[...] = live
    up_edge = jnp.where(below, send_z[5], recv_z[5]) > 0.5

    def ordered(mine, theirs):
        return jnp.where(below, mine, theirs), jnp.where(below, theirs, mine)

    push, drive_here, drive_next = face_terms(
        live,
        ordered(send_z[1], recv_z[1]),
        ordered(send_z[0], recv_z[0]),
        ordered(frac[edge], z_share),
        ordered(slope[edge], z_rise),
        up_edge,
    )
    resid[edge] = resid[edge] + jnp.where(below, push, -push)
    sat_res[edge] = sat_res[edge] + jnp.where(below, drive_here, drive_next)

    hi_share, hi_rise = flow_fraction(recv_hi[2])
    lo_share, lo_rise = flow_fraction(recv_lo[2])
    own_share, own_rise = flow_fraction(send_lo[2])
    low_face = recv_lo[3] * send_lo[3]
    low_push, _, low_drive = face_terms(
        low_face,
        (recv_lo[1], send_lo[1]),
        (recv_lo[0], send_lo[0]),
        (lo_share, own_share),
        (lo_rise, own_rise),
        recv_lo[4] > 0.5,
    )
    hi_press, hi_scaled, hi_act = recv_hi[0], recv_hi[1], recv_hi[3]

    def with_high(value, plane, l):
        return jnp.where(is_high_row, plane[l : l + 1], next_x(value))

    def with_low(value, plane, l):
        return jnp.where(is_low_row, plane[l : l + 1], prev_x(value))

    loads[8].wait()
    for l in range(depth):
        face = trans[1, l] * act[l] * with_high(act[l], hi_act, l)
        push, drive_here, drive_next = face_terms(
            face,
            (scaled[l], with_high(scaled[l], hi_scaled, l)),
            (press[l], with_high(press[l], hi_press, l)),
            (frac[l], with_high(frac[l], hi_share, l)),
            (slope[l], with_high(slope[l], hi_rise, l)),
            (flags[l] & 2) != 0,
        )
        resid[l] = resid[l] + push - with_low(push, low_push, l)
        sat_res[l] = sat_res[l] + drive_here + with_low(drive_next, low_drive, l)
        face_low = with_low(face, low_face, l)
        face_xu[l] = jnp.where(is_high_row, 0.0, face)
        face_xl[l] = jnp.where(is_low_row, 0.0, face_low)
        face_edge[l] = jnp.where(
            is_high_row, face, jnp.where(is_low_row, face_low, 0.0)
        )
        diagonal = comp[l] + face + face_low + face_yu[l] + face_yl[l]
        if l > 0:
            diagonal = diagonal + face_z[l - 1]
        else:
            diagonal = diagonal + jnp.where(below, 0.0, live)
        if l < depth - 1:
            diagonal = diagonal + face_z[l]
        else:
            diagonal = diagonal + jnp.where(below, live, 0.0)
        pivot = diagonal if l == 0 else diagonal - face_z[l - 1] * up_gain[l - 1]
        inverse = 1.0 / pivot
        inv_pivot[l] = inverse
        if l > 0:
            down_gain[l] = face_z[l - 1] * inverse
        if l < depth - 1:
            up_gain[l] = face_z[l] * inverse

    store_sat = pltpu.make_async_copy(sat_res, sat_out, out_sem.at[0])
    store_sat.start()

    def moment(left, right):
        total = None
        for l in range(depth):
            term = left[l] * right[l]
            total = term if total is None else total + term
        return total

    def fold(plane):
        total = plane[:, 0:128]
        for start in range(128, span, 128):
            total = total + plane[:, start : start + 128]
        return jnp.sum(total, axis=0, keepdims=True)

    older = None
    current = [resid[l] for l in range(depth)]
    products = []
    for step in range(ITERS):
        partial = [current[0] * inv_pivot[0]]
        for l in range(1, depth):
            partial.append(current[l] * inv_pivot[l] + down_gain[l] * partial[l - 1])
        vector = [None] * depth
        vector[depth - 1] = partial[depth - 1]
        for l in range(depth - 2, -1, -1):
            vector[l] = partial[l] + up_gain[l] * vector[l + 1]
        for l in range(depth):
            basis[step, l] = vector[l]
            vec_hi[step, l : l + 1] = vector[l][width - 1 : width]
            vec_lo[step, l : l + 1] = vector[l][0:1]
        tags = [3 * step + k for k in range(3)]
        trio = (
            remote(
                vec_hi.at[step], got_lo.at[step],
                vec_send.at[tags[0]], vec_recv.at[tags[0]], upper_id,
            ),
            remote(
                vec_lo.at[step], got_hi.at[step],
                vec_send.at[tags[1]], vec_recv.at[tags[1]], lower_id,
            ),
            remote(
                basis.at[step, edge], got_z.at[step],
                vec_send.at[tags[2]], vec_recv.at[tags[2]], other_id,
            ),
        )
        copies.append(trio)
        exchange(*trio)
        products.append(fold(moment(vector, current)))
        for l in range(depth):
            near = (
                face_xu[l] * next_x(vector[l])
                + face_xl[l] * prev_x(vector[l])
                + face_yu[l] * next_y(vector[l])
                + face_yl[l] * prev_y(vector[l])
            )
            source[l] = near
        arrived(*trio)
        source[edge] = source[edge] + face_zedge[...] * got_z[step]
        later = []
        for l in range(depth):
            halo = jnp.where(
                rows < width // 2, got_lo[step, l : l + 1], got_hi[step, l : l + 1]
            )
            value = source[l] + face_edge[l] * halo
            if step > 0:
                value = 2.0 * value - older[l]
            later.append(value)
        products.append(fold(moment(vector, later)))
        older, current = current, later

    for k, value in enumerate(products):
        sums[0, k : k + 1] = value
    sends = []
    slot = 0
    for place_of, stage in enumerate(stages):
        batch = [
            remote(
                sums.at[place_of], others.at[slot + k],
                sum_send.at[slot + k], sum_recv.at[slot + k], peer_id,
            )
            for k, peer_id in enumerate(stage)
        ]
        for copy in batch:
            copy.start()
        total = sums[place_of]
        for k, copy in enumerate(batch):
            copy.wait_recv()
        for k in range(len(batch)):
            total = total + others[slot + k]
        if place_of + 1 < len(stages):
            sums[place_of + 1] = total
        sends += batch
        slot += len(batch)
    total = jnp.sum(total, axis=1, keepdims=True)
    raw = [total[k : k + 1] for k in range(2 * ITERS)]
    moments = [raw[0], raw[1]]
    for k in range(2, 2 * ITERS):
        moments.append(2.0 * raw[k] - raw[k % 2])
    weights = [jnp.broadcast_to(value, (width, span)) for value in galerkin(moments)]
    for l in range(depth):
        value = weights[0] * basis[0, l]
        for step in range(1, ITERS):
            value = value + weights[step] * basis[step, l]
        sol_res[l] = value
    store_sol = pltpu.make_async_copy(sol_res, sol_out, out_sem.at[1])
    store_sol.start()
    for trio in copies:
        departed(*trio)
    for copy in sends:
        copy.wait_send()
    store_sat.wait()
    store_sol.wait()


def on_device(areal_count, *arrays):
    arrays = list(arrays)
    block = arrays[0].shape
    depth, width, span = block
    wells = arrays[7].shape[0]
    arrays[7] = arrays[7].reshape(1, wells)
    arrays[8] = arrays[8].reshape(1, wells)
    plane = (width, span)
    strip = (depth, span)
    low = min(LOW_GROUP, areal_count)
    slots = low + (areal_count // low - 1)
    f32 = jnp.float32
    cube = pltpu.VMEM(block, f32)

    def vmem(*shape):
        return pltpu.VMEM(shape, f32)

    scratch = [
        cube, cube, cube, cube, cube, vmem(3, *block), pltpu.VMEM(block, jnp.int32),
        pltpu.VMEM((1, wells), jnp.int32), vmem(1, wells),
        cube, cube, cube, cube, cube, cube,
        cube, cube, cube, cube,
        cube, cube, cube, cube, cube, vmem(*plane),
        vmem(ITERS, *block), cube,
        vmem(5, *strip), vmem(4, *strip), vmem(6, *plane),
        vmem(4, *strip), vmem(5, *strip), vmem(6, *plane),
        vmem(ITERS, *strip), vmem(ITERS, *strip),
        vmem(ITERS, *strip), vmem(ITERS, *strip), vmem(ITERS, *plane),
        vmem(3, 2 * ITERS, 128), vmem(slots, 2 * ITERS, 128),
        pltpu.SemaphoreType.DMA((9,)), pltpu.SemaphoreType.DMA((2,)),
        pltpu.SemaphoreType.DMA((3,)), pltpu.SemaphoreType.DMA((3,)),
        pltpu.SemaphoreType.DMA((3 * ITERS,)), pltpu.SemaphoreType.DMA((3 * ITERS,)),
        pltpu.SemaphoreType.DMA((slots,)), pltpu.SemaphoreType.DMA((slots,)),
    ]
    return pl.pallas_call(
        functools.partial(kernel, areal_count),
        out_shape=(jax.ShapeDtypeStruct(block, f32), jax.ShapeDtypeStruct(block, f32)),
        in_specs=[pl.BlockSpec(memory_space=pl.ANY)] * len(arrays),
        out_specs=(pl.BlockSpec(memory_space=pl.ANY), pl.BlockSpec(memory_space=pl.ANY)),
        scratch_shapes=scratch,
        compiler_params=pltpu.CompilerParams(
            collective_id=0, has_side_effects=True, vmem_limit_bytes=60 * 1024 * 1024
        ),
    )(*arrays)


def solution(mesh):
    block = P(("members", "layer"), "areal", None)
    return jax.shard_map(
        functools.partial(on_device, mesh.shape["areal"]),
        mesh=mesh,
        in_specs=(
            block, block, block, block, block,
            P(None, ("members", "layer"), "areal", None),
            block, P("members"), P("members"),
        ),
        out_specs=(block, block),
        check_vma=False,
    )
```

```python
import functools

import jax
import jax.numpy as jnp
from jax import lax
from jax.experimental import pallas as pl
from jax.experimental.pallas import tpu as pltpu
from jax.sharding import PartitionSpec as P

ITERS = 4
MOBILITY_RATIO = 0.5
LOW_GROUP = 8
MESH = pl.DeviceIdType.MESH


def flow_fraction(wetness):
    square = wetness * wetness
    dry = 1.0 - wetness
    inverse = 1.0 / (square + MOBILITY_RATIO * (dry * dry))
    return square * inverse, (2.0 * MOBILITY_RATIO) * wetness * dry * (inverse * inverse)


def face_terms(face, scaled, press, frac, slope, upwind):
    moved = face * (scaled[1] - scaled[0])
    push = moved * jnp.where(upwind, frac[0], frac[1])
    drive = moved * (press[0] - press[1]) * jnp.where(upwind, slope[0], slope[1])
    return push, jnp.where(upwind, drive, 0.0), jnp.where(upwind, 0.0, drive)


def galerkin(moments):
    def inner(i, j):
        return 0.5 * (moments[i + j] + moments[abs(i - j)])

    def entry(i, j):
        moved = inner(i, 1) if j == 0 else 0.5 * (inner(i, j + 1) + inner(i, j - 1))
        return inner(i, j) - moved

    size = ITERS
    lower = [[None] * size for _ in range(size)]
    inverse = []
    forward = []
    for i in range(size):
        for j in range(i):
            total = entry(i, j)
            for k in range(j):
                total = total - lower[i][k] * lower[j][k] * inverse[k]
            lower[i][j] = total
        diagonal = entry(i, i)
        pivot = diagonal
        right = moments[i]
        for k in range(i):
            scale = lower[i][k] * inverse[k]
            pivot = pivot - scale * lower[i][k]
            right = right - scale * forward[k]
        keep = pivot > 1e-6 * diagonal
        inv = jnp.where(keep, 1.0 / jnp.where(keep, pivot, 1.0), 0.0)
        inverse.append(inv)
        forward.append(right)
    solved = [None] * size
    for i in range(size - 1, -1, -1):
        total = forward[i]
        for k in range(i + 1, size):
            total = total - lower[k][i] * solved[k]
        solved[i] = total * inverse[i]
    return solved


def kernel(
    areal_count,
    press_in, wet_in, cot_in, dt_in, comp_in, trans_in, flags_in, cells_in, misfit_in,
    sat_out, sol_out,
    press, wet, cot, dt, comp, trans, flags, cells, misfit,
    scaled, frac, slope, resid, sat_res, sol_res,
    face_z, inv_pivot, down_gain, up_gain,
    face_xu, face_xl, face_yu, face_yl, face_edge, face_zedge,
    basis, source,
    send_hi, send_lo, send_z, recv_hi, recv_lo, recv_z,
    vec_hi, vec_lo, got_hi, got_lo, got_z,
    coef_hi, coef_lo, got_coef_hi, got_coef_lo, edge_face,
    diag_hi, diag_lo, got_diag_hi, got_diag_lo,
    sums, others,
    in_sem, out_sem, face_send, face_recv, vec_send, vec_recv, sum_send, sum_recv,
):
    depth, width, span = press.shape
    areal = lax.axis_index("areal")
    layer = lax.axis_index("layer")
    has_lo = areal > 0
    has_hi = areal < areal_count - 1
    lower_id = {"areal": jnp.maximum(areal - 1, 0), "layer": layer}
    upper_id = {"areal": jnp.minimum(areal + 1, areal_count - 1), "layer": layer}
    other_id = {"areal": areal, "layer": 1 - layer}
    lower_diag = {"areal": jnp.maximum(areal - 1, 0), "layer": 1 - layer}
    upper_diag = {"areal": jnp.minimum(areal + 1, areal_count - 1), "layer": 1 - layer}
    edge = (depth - 1) * (1 - layer)

    low = min(LOW_GROUP, areal_count)
    high = areal_count // low
    place = lax.rem(areal, low)
    first = areal - place
    stages = [
        [other_id],
        [
            {"areal": first + lax.rem(place + step, low), "layer": layer}
            for step in range(1, low)
        ],
    ]
    if high > 1:
        row = lax.div(areal, low)
        stages.append(
            [
                {"areal": lax.rem(row + step, high) * low + place, "layer": layer}
                for step in range(1, high)
            ]
        )

    pairs = [
        (cells_in, cells), (misfit_in, misfit), (cot_in, cot), (dt_in, dt), (flags_in, flags),
        (press_in, press), (wet_in, wet), (trans_in, trans), (comp_in, comp),
    ]
    loads = [
        pltpu.make_async_copy(src, dst, in_sem.at[place_of])
        for place_of, (src, dst) in enumerate(pairs)
    ]
    for load in loads:
        load.start()

    barrier = pltpu.get_barrier_semaphore()
    for stage in stages:
        for peer_id in stage:
            pl.semaphore_signal(barrier, inc=1, device_id=peer_id, device_id_type=MESH)
    expected = sum(len(stage) for stage in stages)
    beside = 2 if high > 1 else 1

    @pl.when(has_lo)
    def _():
        for peer_id in (lower_diag, lower_id)[:beside]:
            pl.semaphore_signal(barrier, inc=1, device_id=peer_id, device_id_type=MESH)

    @pl.when(has_hi)
    def _():
        for peer_id in (upper_diag, upper_id)[:beside]:
            pl.semaphore_signal(barrier, inc=1, device_id=peer_id, device_id_type=MESH)

    @pl.when(jnp.logical_not(has_lo))
    def _():
        recv_lo[...] = jnp.zeros_like(recv_lo)
        got_lo[...] = jnp.zeros_like(got_lo)
        got_coef_lo[...] = jnp.zeros_like(got_coef_lo)
        got_diag_lo[...] = jnp.zeros_like(got_diag_lo)

    @pl.when(jnp.logical_not(has_hi))
    def _():
        recv_hi[...] = jnp.zeros_like(recv_hi)
        got_hi[...] = jnp.zeros_like(got_hi)
        got_coef_hi[...] = jnp.zeros_like(got_coef_hi)
        got_diag_hi[...] = jnp.zeros_like(got_diag_hi)

    rows = lax.broadcasted_iota(jnp.int32, (width, span), 0)
    lanes = lax.broadcasted_iota(jnp.int32, (width, span), 1)
    is_low_row = rows == 0
    is_high_row = rows == width - 1
    is_last_lane = lanes == span - 1
    strip_rows = lax.broadcasted_iota(jnp.int32, (depth, span), 0)

    def next_y(value):
        return pltpu.roll(value, span - 1, 1)

    def prev_y(value):
        return pltpu.roll(value, 1, 1)

    def next_x(value):
        return pltpu.roll(value, width - 1, 0)

    def prev_x(value):
        return pltpu.roll(value, 1, 0)

    loads[0].wait()
    loads[1].wait()
    cell = cells[...]
    wells = cell.shape[1]
    local = lax.broadcasted_iota(jnp.int32, (depth * width, wells), 0)
    base = (
        (layer * depth + lax.shift_right_logical(local, (width - 1).bit_length()))
        * (areal_count * width)
        + areal * width + lax.bitwise_and(local, width - 1)
    ) * span
    offset = cell - base
    by_row = jnp.where((offset >= 0) & (offset < span), misfit[...], 0.0)
    lane_of = lax.bitwise_and(cell, span - 1)
    by_lane = jnp.where(
        lax.broadcasted_iota(jnp.int32, (span, wells), 0) == lane_of, 1.0, 0.0
    )
    added = lax.dot_general(
        by_row, by_lane, (((1,), (1,)), ((), ())),
        precision=lax.Precision.HIGHEST, preferred_element_type=jnp.float32,
    )
    for load in loads[2:8]:
        load.wait()
    act = []
    for l in range(depth):
        modified = cot[l] + added[l * width : (l + 1) * width]
        sat_res[l] = modified
        scaled[l] = dt[l] * modified
        act.append(jnp.where((flags[l] & 8) != 0, 1.0, 0.0))

    for l in range(depth):
        here = slice(l, l + 1)
        top = slice(width - 1, width)
        live_x = trans[1, l] * act[l]
        up_x = jnp.where((flags[l] & 2) != 0, 1.0, 0.0)
        for k, plane in enumerate((press[l], scaled[l], wet[l], live_x, up_x)):
            send_hi[k, here] = plane[top]
        for k, plane in enumerate((press[l], scaled[l], wet[l], act[l])):
            send_lo[k, here] = plane[0:1]
    edge_act = jnp.where((flags[edge] & 8) != 0, 1.0, 0.0)
    send_z[0] = press[edge]
    send_z[1] = scaled[edge]
    send_z[2] = wet[edge]
    send_z[3] = edge_act
    send_z[4] = trans[0, edge] * edge_act
    send_z[5] = jnp.where((flags[edge] & 1) != 0, 1.0, 0.0)

    sides_there = jnp.where(has_lo, 1, 0) + jnp.where(has_hi, 1, 0)
    pl.semaphore_wait(barrier, expected + beside * sides_there)

    def remote(src, dst, send_sem, recv_sem, target):
        return pltpu.make_async_remote_copy(
            src_ref=src, dst_ref=dst, send_sem=send_sem, recv_sem=recv_sem,
            device_id=target, device_id_type=MESH,
        )

    def exchange(ups, lows, across):
        if ups:
            @pl.when(has_hi)
            def _():
                for copy in ups:
                    copy.start()

            @pl.when(has_lo)
            def _():
                for copy in lows:
                    copy.start()

        for copy in across:
            copy.start()

    def arrived(ups, lows, across):
        for copy in across:
            copy.wait_recv()
        if ups:
            @pl.when(has_lo)
            def _():
                for copy in ups:
                    copy.wait_recv()

            @pl.when(has_hi)
            def _():
                for copy in lows:
                    copy.wait_recv()

    def departed(ups, lows, across):
        for copy in across:
            copy.wait_send()
        if ups:
            @pl.when(has_hi)
            def _():
                for copy in ups:
                    copy.wait_send()

            @pl.when(has_lo)
            def _():
                for copy in lows:
                    copy.wait_send()

    copies = [
        (
            [remote(send_hi, recv_lo, face_send.at[0], face_recv.at[0], upper_id)],
            [remote(send_lo, recv_hi, face_send.at[1], face_recv.at[1], lower_id)],
            [remote(send_z, recv_z, face_send.at[2], face_recv.at[2], other_id)],
        )
    ]
    exchange(*copies[0])

    for l in range(depth):
        share, rise = flow_fraction(wet[l])
        frac[l] = share
        slope[l] = rise
    carried = None
    for l in range(depth):
        up = (flags[l] & 4) != 0
        face = jnp.where(is_last_lane, 0.0, trans[2, l] * act[l] * next_y(act[l]))
        face_yu[l] = face
        face_yl[l] = prev_y(face)
        push, drive_here, drive_next = face_terms(
            face,
            (scaled[l], next_y(scaled[l])),
            (press[l], next_y(press[l])),
            (frac[l], next_y(frac[l])),
            (slope[l], next_y(slope[l])),
            up,
        )
        pushed = push - prev_y(push)
        driven = sat_res[l] + drive_here + prev_y(drive_next)
        if carried is not None:
            pushed = pushed - carried[0]
            driven = driven + carried[1]
        if l < depth - 1:
            face = trans[0, l] * act[l] * act[l + 1]
            face_z[l] = face
            push, drive_here, drive_next = face_terms(
                face,
                (scaled[l], scaled[l + 1]),
                (press[l], press[l + 1]),
                (frac[l], frac[l + 1]),
                (slope[l], slope[l + 1]),
                (flags[l] & 1) != 0,
            )
            pushed = pushed + push
            driven = driven + drive_here
            carried = (push, drive_next)
        resid[l] = pushed
        sat_res[l] = driven

    arrived(*copies[0])

    below = layer == 0
    z_share, z_rise = flow_fraction(recv_z[2])
    live = jnp.where(below, trans[0, edge] * edge_act * recv_z[3], recv_z[4] * edge_act)
    face_zedge[...] = live
    up_edge = jnp.where(below, send_z[5], recv_z[5]) > 0.5

    def ordered(mine, theirs):
        return jnp.where(below, mine, theirs), jnp.where(below, theirs, mine)

    push, drive_here, drive_next = face_terms(
        live,
        ordered(send_z[1], recv_z[1]),
        ordered(send_z[0], recv_z[0]),
        ordered(frac[edge], z_share),
        ordered(slope[edge], z_rise),
        up_edge,
    )
    resid[edge] = resid[edge] + jnp.where(below, push, -push)
    sat_res[edge] = sat_res[edge] + jnp.where(below, drive_here, drive_next)

    hi_share, hi_rise = flow_fraction(recv_hi[2])
    lo_share, lo_rise = flow_fraction(recv_lo[2])
    own_share, own_rise = flow_fraction(send_lo[2])
    low_face = recv_lo[3] * send_lo[3]
    low_push, _, low_drive = face_terms(
        low_face,
        (recv_lo[1], send_lo[1]),
        (recv_lo[0], send_lo[0]),
        (lo_share, own_share),
        (lo_rise, own_rise),
        recv_lo[4] > 0.5,
    )
    hi_press, hi_scaled, hi_act = recv_hi[0], recv_hi[1], recv_hi[3]

    def with_high(value, plane, l):
        return jnp.where(is_high_row, plane[l : l + 1], next_x(value))

    def with_low(value, plane, l):
        return jnp.where(is_low_row, plane[l : l + 1], prev_x(value))

    loads[8].wait()
    for l in range(depth):
        face = trans[1, l] * act[l] * with_high(act[l], hi_act, l)
        push, drive_here, drive_next = face_terms(
            face,
            (scaled[l], with_high(scaled[l], hi_scaled, l)),
            (press[l], with_high(press[l], hi_press, l)),
            (frac[l], with_high(frac[l], hi_share, l)),
            (slope[l], with_high(slope[l], hi_rise, l)),
            (flags[l] & 2) != 0,
        )
        resid[l] = resid[l] + push - with_low(push, low_push, l)
        sat_res[l] = sat_res[l] + drive_here + with_low(drive_next, low_drive, l)
        face_low = with_low(face, low_face, l)
        face_xu[l] = jnp.where(is_high_row, 0.0, face)
        face_xl[l] = jnp.where(is_low_row, 0.0, face_low)
        face_edge[l] = jnp.where(
            is_high_row, face, jnp.where(is_low_row, face_low, 0.0)
        )
        diagonal = comp[l] + face + face_low + face_yu[l] + face_yl[l]
        if l > 0:
            diagonal = diagonal + face_z[l - 1]
        else:
            diagonal = diagonal + jnp.where(below, 0.0, live)
        if l < depth - 1:
            diagonal = diagonal + face_z[l]
        else:
            diagonal = diagonal + jnp.where(below, live, 0.0)
        pivot = diagonal if l == 0 else diagonal - face_z[l - 1] * up_gain[l - 1]
        inverse = 1.0 / pivot
        inv_pivot[l] = inverse
        if l > 0:
            down_gain[l] = face_z[l - 1] * inverse
        if l < depth - 1:
            up_gain[l] = face_z[l] * inverse
        here = slice(l, l + 1)
        joint = face_z[l] if l < depth - 1 else live
        edge_face[here] = face[width - 1 : width]
        for k, plane in enumerate((face_low, face_yu[l], inverse, joint)):
            coef_hi[k, here] = plane[width - 1 : width]
        for k, plane in enumerate((face, face_yu[l], inverse, joint)):
            coef_lo[k, here] = plane[0:1]

    store_sat = pltpu.make_async_copy(sat_res, sat_out, out_sem.at[0])
    store_sat.start()

    def moment(left, right):
        total = None
        for l in range(depth):
            term = left[l] * right[l]
            total = term if total is None else total + term
        return total

    def fold(plane):
        total = plane[:, 0:128]
        for start in range(128, span, 128):
            total = total + plane[:, start : start + 128]
        return jnp.sum(total, axis=0, keepdims=True)

    older = None
    current = [resid[l] for l in range(depth)]
    products = []
    for step in range(ITERS):
        partial = [current[0] * inv_pivot[0]]
        for l in range(1, depth):
            partial.append(current[l] * inv_pivot[l] + down_gain[l] * partial[l - 1])
        vector = [None] * depth
        vector[depth - 1] = partial[depth - 1]
        for l in range(depth - 2, -1, -1):
            vector[l] = partial[l] + up_gain[l] * vector[l + 1]
        wide = step % 2 == 0
        for l in range(depth):
            basis[step, l] = vector[l]
            if wide:
                here = slice(l, l + 1)
                vec_hi[step, 0, here] = vector[l][width - 1 : width]
                vec_hi[step, 1, here] = vector[l][width - 2 : width - 1]
                vec_lo[step, 0, here] = vector[l][0:1]
                vec_lo[step, 1, here] = vector[l][1:2]
        tag = 8 * step

        def hop(src, dst, target):
            nonlocal tag
            tag += 1
            return remote(src, dst, vec_send.at[tag - 1], vec_recv.at[tag - 1], target)

        ups, lows = [], []
        if wide:
            outer = basis[step, edge]
            diag_hi[step] = outer[width - 1 : width]
            diag_lo[step] = outer[0:1]
            ups = [
                hop(vec_hi.at[step], got_lo.at[step], upper_id),
                hop(diag_hi.at[step], got_diag_lo.at[step], upper_diag),
            ]
            lows = [
                hop(vec_lo.at[step], got_hi.at[step], lower_id),
                hop(diag_lo.at[step], got_diag_hi.at[step], lower_diag),
            ]
        trio = (ups, lows, [hop(basis.at[step, edge], got_z.at[step], other_id)])
        copies.append(trio)
        exchange(*trio)
        if step == 0:
            coefs = (
                [hop(coef_hi, got_coef_lo, upper_id)],
                [hop(coef_lo, got_coef_hi, lower_id)],
                [],
            )
            copies.append(coefs)
            exchange(*coefs)
        products.append(fold(moment(vector, current)))
        for l in range(depth):
            near = (
                face_xu[l] * next_x(vector[l])
                + face_xl[l] * prev_x(vector[l])
                + face_yu[l] * next_y(vector[l])
                + face_yl[l] * prev_y(vector[l])
            )
            source[l] = near
        arrived(*trio)
        source[edge] = source[edge] + face_zedge[...] * got_z[step]
        later = []
        for l in range(depth):
            halo = jnp.where(
                rows < width // 2, got_lo[step, 0, l : l + 1], got_hi[step, 0, l : l + 1]
            )
            value = source[l] + face_edge[l] * halo
            if step > 0:
                value = 2.0 * value - older[l]
            later.append(value)
        products.append(fold(moment(vector, later)))
        if wide:
            if step == 0:
                arrived(*coefs)
                halo_old = [None, None]
            sides = (
                (got_lo, vec_lo, got_coef_lo, got_diag_lo, recv_lo[3] * send_lo[3]),
                (got_hi, vec_hi, got_coef_hi, got_diag_hi, edge_face[...]),
            )
            for side, (got, own, coef, diag, between) in enumerate(sides):
                beside_it = got[step, 0]
                value = (
                    coef[0] * got[step, 1]
                    + between * own[step, 0]
                    + coef[1] * next_y(beside_it)
                    + prev_y(coef[1] * beside_it)
                )
                joint = coef[3, depth - 1 : depth]
                value = value + jnp.where(strip_rows == edge, joint * diag[step], 0.0)
                if step > 0:
                    value = 2.0 * value - halo_old[side]
                halo_old[side] = value
                inverse = coef[2]
                scaled_value = value * inverse
                gain_up = coef[3] * inverse
                part = [scaled_value[0:1]]
                for l in range(1, depth):
                    gain = coef[3, l - 1 : l] * inverse[l : l + 1]
                    part.append(scaled_value[l : l + 1] + gain * part[l - 1])
                solved = part[depth - 1]
                got[step + 1, 0, depth - 1 : depth] = solved
                for l in range(depth - 2, -1, -1):
                    solved = part[l] + gain_up[l : l + 1] * solved
                    got[step + 1, 0, l : l + 1] = solved
        older, current = current, later

    for k, value in enumerate(products):
        sums[0, k : k + 1] = value
    sends = []
    slot = 0
    for place_of, stage in enumerate(stages):
        batch = [
            remote(
                sums.at[place_of], others.at[slot + k],
                sum_send.at[slot + k], sum_recv.at[slot + k], peer_id,
            )
            for k, peer_id in enumerate(stage)
        ]
        for copy in batch:
            copy.start()
        total = sums[place_of]
        for k, copy in enumerate(batch):
            copy.wait_recv()
        for k in range(len(batch)):
            total = total + others[slot + k]
        if place_of + 1 < len(stages):
            sums[place_of + 1] = total
        sends += batch
        slot += len(batch)
    total = jnp.sum(total, axis=1, keepdims=True)
    raw = [total[k : k + 1] for k in range(2 * ITERS)]
    moments = [raw[0], raw[1]]
    for k in range(2, 2 * ITERS):
        moments.append(2.0 * raw[k] - raw[k % 2])
    weights = [jnp.broadcast_to(value, (width, span)) for value in galerkin(moments)]
    for l in range(depth):
        value = weights[0] * basis[0, l]
        for step in range(1, ITERS):
            value = value + weights[step] * basis[step, l]
        sol_res[l] = value
    store_sol = pltpu.make_async_copy(sol_res, sol_out, out_sem.at[1])
    store_sol.start()
    for trio in copies:
        departed(*trio)
    for copy in sends:
        copy.wait_send()
    store_sat.wait()
    store_sol.wait()


def on_device(areal_count, *arrays):
    arrays = list(arrays)
    block = arrays[0].shape
    depth, width, span = block
    wells = arrays[7].shape[0]
    arrays[7] = arrays[7].reshape(1, wells)
    arrays[8] = arrays[8].reshape(1, wells)
    plane = (width, span)
    strip = (depth, span)
    low = min(LOW_GROUP, areal_count)
    slots = low + (areal_count // low - 1)
    f32 = jnp.float32
    cube = pltpu.VMEM(block, f32)

    def vmem(*shape):
        return pltpu.VMEM(shape, f32)

    scratch = [
        cube, cube, cube, cube, cube, vmem(3, *block), pltpu.VMEM(block, jnp.int32),
        pltpu.VMEM((1, wells), jnp.int32), vmem(1, wells),
        cube, cube, cube, cube, cube, cube,
        cube, cube, cube, cube,
        cube, cube, cube, cube, cube, vmem(*plane),
        vmem(ITERS, *block), cube,
        vmem(5, *strip), vmem(4, *strip), vmem(6, *plane),
        vmem(4, *strip), vmem(5, *strip), vmem(6, *plane),
        vmem(ITERS, 2, *strip), vmem(ITERS, 2, *strip),
        vmem(ITERS, 2, *strip), vmem(ITERS, 2, *strip), vmem(ITERS, *plane),
        vmem(4, *strip), vmem(4, *strip), vmem(4, *strip), vmem(4, *strip), vmem(*strip),
        vmem(ITERS, 1, span), vmem(ITERS, 1, span), vmem(ITERS, 1, span), vmem(ITERS, 1, span),
        vmem(3, 2 * ITERS, 128), vmem(slots, 2 * ITERS, 128),
        pltpu.SemaphoreType.DMA((9,)), pltpu.SemaphoreType.DMA((2,)),
        pltpu.SemaphoreType.DMA((3,)), pltpu.SemaphoreType.DMA((3,)),
        pltpu.SemaphoreType.DMA((8 * ITERS,)), pltpu.SemaphoreType.DMA((8 * ITERS,)),
        pltpu.SemaphoreType.DMA((slots,)), pltpu.SemaphoreType.DMA((slots,)),
    ]
    return pl.pallas_call(
        functools.partial(kernel, areal_count),
        out_shape=(jax.ShapeDtypeStruct(block, f32), jax.ShapeDtypeStruct(block, f32)),
        in_specs=[pl.BlockSpec(memory_space=pl.ANY)] * len(arrays),
        out_specs=(pl.BlockSpec(memory_space=pl.ANY), pl.BlockSpec(memory_space=pl.ANY)),
        scratch_shapes=scratch,
        compiler_params=pltpu.CompilerParams(
            collective_id=0, has_side_effects=True, vmem_limit_bytes=60 * 1024 * 1024
        ),
    )(*arrays)


def solution(mesh):
    block = P(("members", "layer"), "areal", None)
    return jax.shard_map(
        functools.partial(on_device, mesh.shape["areal"]),
        mesh=mesh,
        in_specs=(
            block, block, block, block, block,
            P(None, ("members", "layer"), "areal", None),
            block, P("members"), P("members"),
        ),
        out_specs=(block, block),
        check_vma=False,
    )
```

```python
import functools

import jax
import jax.numpy as jnp
from jax import lax
from jax.experimental import pallas as pl
from jax.experimental.pallas import tpu as pltpu
from jax.sharding import PartitionSpec as P

ITERS = 4
MOBILITY_RATIO = 0.5
LOW_GROUP = 8
MESH = pl.DeviceIdType.MESH


def flow_fraction(wetness):
    square = wetness * wetness
    dry = 1.0 - wetness
    inverse = 1.0 / (square + MOBILITY_RATIO * (dry * dry))
    return square * inverse, (2.0 * MOBILITY_RATIO) * wetness * dry * (inverse * inverse)


def face_terms(face, scaled, press, frac, slope, upwind):
    moved = face * (scaled[1] - scaled[0])
    push = moved * jnp.where(upwind, frac[0], frac[1])
    drive = moved * (press[0] - press[1]) * jnp.where(upwind, slope[0], slope[1])
    return push, jnp.where(upwind, drive, 0.0), jnp.where(upwind, 0.0, drive)


def galerkin(moments):
    def inner(i, j):
        return 0.5 * (moments[i + j] + moments[abs(i - j)])

    def entry(i, j):
        moved = inner(i, 1) if j == 0 else 0.5 * (inner(i, j + 1) + inner(i, j - 1))
        return inner(i, j) - moved

    size = ITERS
    lower = [[None] * size for _ in range(size)]
    inverse = []
    forward = []
    for i in range(size):
        for j in range(i):
            total = entry(i, j)
            for k in range(j):
                total = total - lower[i][k] * lower[j][k] * inverse[k]
            lower[i][j] = total
        diagonal = entry(i, i)
        pivot = diagonal
        right = moments[i]
        for k in range(i):
            scale = lower[i][k] * inverse[k]
            pivot = pivot - scale * lower[i][k]
            right = right - scale * forward[k]
        keep = pivot > 1e-6 * diagonal
        inv = jnp.where(keep, 1.0 / jnp.where(keep, pivot, 1.0), 0.0)
        inverse.append(inv)
        forward.append(right)
    solved = [None] * size
    for i in range(size - 1, -1, -1):
        total = forward[i]
        for k in range(i + 1, size):
            total = total - lower[k][i] * solved[k]
        solved[i] = total * inverse[i]
    return solved


def kernel(
    areal_count,
    press_in, wet_in, cot_in, dt_in, comp_in, trans_in, flags_in, cells_in, misfit_in,
    sat_out, sol_out,
    press, wet, cot, dt, comp, trans, flags, cells, misfit,
    scaled, frac, slope, resid, sat_res, sol_res,
    face_z, inv_pivot, down_gain, up_gain,
    face_xu, face_xl, face_yu, face_yl, face_edge, face_zedge,
    basis, source,
    send_hi, send_lo, send_z, recv_hi, recv_lo, recv_z,
    vec_hi, vec_lo, got_hi, got_lo, got_z,
    coef_hi, coef_lo, got_coef_hi, got_coef_lo, edge_face,
    diag_hi, diag_lo, got_diag_hi, got_diag_lo,
    sums, others,
    in_sem, out_sem, face_send, face_recv, vec_send, vec_recv, sum_send, sum_recv,
):
    depth, width, span = press.shape
    areal = lax.axis_index("areal")
    layer = lax.axis_index("layer")
    has_lo = areal > 0
    has_hi = areal < areal_count - 1
    lower_id = {"areal": jnp.maximum(areal - 1, 0), "layer": layer}
    upper_id = {"areal": jnp.minimum(areal + 1, areal_count - 1), "layer": layer}
    other_id = {"areal": areal, "layer": 1 - layer}
    lower_diag = {"areal": jnp.maximum(areal - 1, 0), "layer": 1 - layer}
    upper_diag = {"areal": jnp.minimum(areal + 1, areal_count - 1), "layer": 1 - layer}
    edge = (depth - 1) * (1 - layer)

    low = min(LOW_GROUP, areal_count)
    high = areal_count // low
    place = lax.rem(areal, low)
    first = areal - place
    stages = [
        [other_id],
        [
            {"areal": first + lax.rem(place + step, low), "layer": layer}
            for step in range(1, low)
        ],
    ]
    if high > 1:
        row = lax.div(areal, low)
        stages.append(
            [
                {"areal": lax.rem(row + step, high) * low + place, "layer": layer}
                for step in range(1, high)
            ]
        )

    pairs = [
        (cells_in, cells), (misfit_in, misfit), (cot_in, cot), (dt_in, dt), (flags_in, flags),
        (press_in, press), (wet_in, wet), (trans_in, trans), (comp_in, comp),
    ]
    loads = [
        pltpu.make_async_copy(src, dst, in_sem.at[place_of])
        for place_of, (src, dst) in enumerate(pairs)
    ]
    for load in loads:
        load.start()

    barrier = pltpu.get_barrier_semaphore()
    for stage in stages:
        for peer_id in stage:
            pl.semaphore_signal(barrier, inc=1, device_id=peer_id, device_id_type=MESH)
    expected = sum(len(stage) for stage in stages)
    beside = 2 if high > 1 else 1

    @pl.when(has_lo)
    def _():
        for peer_id in (lower_diag, lower_id)[:beside]:
            pl.semaphore_signal(barrier, inc=1, device_id=peer_id, device_id_type=MESH)

    @pl.when(has_hi)
    def _():
        for peer_id in (upper_diag, upper_id)[:beside]:
            pl.semaphore_signal(barrier, inc=1, device_id=peer_id, device_id_type=MESH)

    @pl.when(jnp.logical_not(has_lo))
    def _():
        recv_lo[...] = jnp.zeros_like(recv_lo)
        got_lo[...] = jnp.zeros_like(got_lo)
        got_coef_lo[...] = jnp.zeros_like(got_coef_lo)
        got_diag_lo[...] = jnp.zeros_like(got_diag_lo)

    @pl.when(jnp.logical_not(has_hi))
    def _():
        recv_hi[...] = jnp.zeros_like(recv_hi)
        got_hi[...] = jnp.zeros_like(got_hi)
        got_coef_hi[...] = jnp.zeros_like(got_coef_hi)
        got_diag_hi[...] = jnp.zeros_like(got_diag_hi)

    rows = lax.broadcasted_iota(jnp.int32, (width, span), 0)
    lanes = lax.broadcasted_iota(jnp.int32, (width, span), 1)
    is_low_row = rows == 0
    is_high_row = rows == width - 1
    is_last_lane = lanes == span - 1
    strip_rows = lax.broadcasted_iota(jnp.int32, (depth, span), 0)

    def next_y(value):
        return pltpu.roll(value, span - 1, 1)

    def prev_y(value):
        return pltpu.roll(value, 1, 1)

    def next_x(value):
        return pltpu.roll(value, width - 1, 0)

    def prev_x(value):
        return pltpu.roll(value, 1, 0)

    loads[0].wait()
    loads[1].wait()
    cell = cells[...]
    wells = cell.shape[1]
    local = lax.broadcasted_iota(jnp.int32, (depth * width, wells), 0)
    base = (
        (layer * depth + lax.shift_right_logical(local, (width - 1).bit_length()))
        * (areal_count * width)
        + areal * width + lax.bitwise_and(local, width - 1)
    ) * span
    offset = cell - base
    by_row = jnp.where((offset >= 0) & (offset < span), misfit[...], 0.0)
    lane_of = lax.bitwise_and(cell, span - 1)
    by_lane = jnp.where(
        lax.broadcasted_iota(jnp.int32, (span, wells), 0) == lane_of, 1.0, 0.0
    )
    added = lax.dot_general(
        by_row, by_lane, (((1,), (1,)), ((), ())),
        precision=lax.Precision.HIGHEST, preferred_element_type=jnp.float32,
    )
    for load in loads[2:8]:
        load.wait()
    act = []
    for l in range(depth):
        modified = cot[l] + added[l * width : (l + 1) * width]
        sat_res[l] = modified
        scaled[l] = dt[l] * modified
        act.append(jnp.where((flags[l] & 8) != 0, 1.0, 0.0))

    for l in range(depth):
        here = slice(l, l + 1)
        top = slice(width - 1, width)
        live_x = trans[1, l] * act[l]
        up_x = jnp.where((flags[l] & 2) != 0, 1.0, 0.0)
        for k, plane in enumerate((press[l], scaled[l], wet[l], live_x, up_x)):
            send_hi[k, here] = plane[top]
        for k, plane in enumerate((press[l], scaled[l], wet[l], act[l])):
            send_lo[k, here] = plane[0:1]
    edge_act = jnp.where((flags[edge] & 8) != 0, 1.0, 0.0)
    send_z[0] = press[edge]
    send_z[1] = scaled[edge]
    send_z[2] = wet[edge]
    send_z[3] = edge_act
    send_z[4] = trans[0, edge] * edge_act
    send_z[5] = jnp.where((flags[edge] & 1) != 0, 1.0, 0.0)

    sides_there = jnp.where(has_lo, 1, 0) + jnp.where(has_hi, 1, 0)
    pl.semaphore_wait(barrier, expected + beside * sides_there)

    def remote(src, dst, send_sem, recv_sem, target):
        return pltpu.make_async_remote_copy(
            src_ref=src, dst_ref=dst, send_sem=send_sem, recv_sem=recv_sem,
            device_id=target, device_id_type=MESH,
        )

    def exchange(ups, lows, across):
        if ups:
            @pl.when(has_hi)
            def _():
                for copy in ups:
                    copy.start()

            @pl.when(has_lo)
            def _():
                for copy in lows:
                    copy.start()

        for copy in across:
            copy.start()

    def arrived(ups, lows, across):
        for copy in across:
            copy.wait_recv()
        if ups:
            @pl.when(has_lo)
            def _():
                for copy in ups:
                    copy.wait_recv()

            @pl.when(has_hi)
            def _():
                for copy in lows:
                    copy.wait_recv()

    def departed(ups, lows, across):
        for copy in across:
            copy.wait_send()
        if ups:
            @pl.when(has_hi)
            def _():
                for copy in ups:
                    copy.wait_send()

            @pl.when(has_lo)
            def _():
                for copy in lows:
                    copy.wait_send()

    copies = [
        (
            [remote(send_hi, recv_lo, face_send.at[0], face_recv.at[0], upper_id)],
            [remote(send_lo, recv_hi, face_send.at[1], face_recv.at[1], lower_id)],
            [remote(send_z, recv_z, face_send.at[2], face_recv.at[2], other_id)],
        )
    ]
    exchange(*copies[0])

    for l in range(depth):
        share, rise = flow_fraction(wet[l])
        frac[l] = share
        slope[l] = rise
    carried = None
    for l in range(depth):
        up = (flags[l] & 4) != 0
        face = jnp.where(is_last_lane, 0.0, trans[2, l] * act[l] * next_y(act[l]))
        face_yu[l] = face
        face_yl[l] = prev_y(face)
        push, drive_here, drive_next = face_terms(
            face,
            (scaled[l], next_y(scaled[l])),
            (press[l], next_y(press[l])),
            (frac[l], next_y(frac[l])),
            (slope[l], next_y(slope[l])),
            up,
        )
        pushed = push - prev_y(push)
        driven = sat_res[l] + drive_here + prev_y(drive_next)
        if carried is not None:
            pushed = pushed - carried[0]
            driven = driven + carried[1]
        if l < depth - 1:
            face = trans[0, l] * act[l] * act[l + 1]
            face_z[l] = face
            push, drive_here, drive_next = face_terms(
                face,
                (scaled[l], scaled[l + 1]),
                (press[l], press[l + 1]),
                (frac[l], frac[l + 1]),
                (slope[l], slope[l + 1]),
                (flags[l] & 1) != 0,
            )
            pushed = pushed + push
            driven = driven + drive_here
            carried = (push, drive_next)
        resid[l] = pushed
        sat_res[l] = driven

    arrived(*copies[0])

    below = layer == 0
    z_share, z_rise = flow_fraction(recv_z[2])
    live = jnp.where(below, trans[0, edge] * edge_act * recv_z[3], recv_z[4] * edge_act)
    face_zedge[...] = live
    up_edge = jnp.where(below, send_z[5], recv_z[5]) > 0.5

    def ordered(mine, theirs):
        return jnp.where(below, mine, theirs), jnp.where(below, theirs, mine)

    push, drive_here, drive_next = face_terms(
        live,
        ordered(send_z[1], recv_z[1]),
        ordered(send_z[0], recv_z[0]),
        ordered(frac[edge], z_share),
        ordered(slope[edge], z_rise),
        up_edge,
    )
    resid[edge] = resid[edge] + jnp.where(below, push, -push)
    sat_res[edge] = sat_res[edge] + jnp.where(below, drive_here, drive_next)

    hi_share, hi_rise = flow_fraction(recv_hi[2])
    lo_share, lo_rise = flow_fraction(recv_lo[2])
    own_share, own_rise = flow_fraction(send_lo[2])
    low_face = recv_lo[3] * send_lo[3]
    low_push, _, low_drive = face_terms(
        low_face,
        (recv_lo[1], send_lo[1]),
        (recv_lo[0], send_lo[0]),
        (lo_share, own_share),
        (lo_rise, own_rise),
        recv_lo[4] > 0.5,
    )
    hi_press, hi_scaled, hi_act = recv_hi[0], recv_hi[1], recv_hi[3]

    def with_high(value, plane, l):
        return jnp.where(is_high_row, plane[l : l + 1], next_x(value))

    def with_low(value, plane, l):
        return jnp.where(is_low_row, plane[l : l + 1], prev_x(value))

    loads[8].wait()
    for l in range(depth):
        face = trans[1, l] * act[l] * with_high(act[l], hi_act, l)
        push, drive_here, drive_next = face_terms(
            face,
            (scaled[l], with_high(scaled[l], hi_scaled, l)),
            (press[l], with_high(press[l], hi_press, l)),
            (frac[l], with_high(frac[l], hi_share, l)),
            (slope[l], with_high(slope[l], hi_rise, l)),
            (flags[l] & 2) != 0,
        )
        resid[l] = resid[l] + push - with_low(push, low_push, l)
        sat_res[l] = sat_res[l] + drive_here + with_low(drive_next, low_drive, l)
        face_low = with_low(face, low_face, l)
        face_xu[l] = jnp.where(is_high_row, 0.0, face)
        face_xl[l] = jnp.where(is_low_row, 0.0, face_low)
        face_edge[l] = jnp.where(
            is_high_row, face, jnp.where(is_low_row, face_low, 0.0)
        )
        diagonal = comp[l] + face + face_low + face_yu[l] + face_yl[l]
        if l > 0:
            diagonal = diagonal + face_z[l - 1]
        else:
            diagonal = diagonal + jnp.where(below, 0.0, live)
        if l < depth - 1:
            diagonal = diagonal + face_z[l]
        else:
            diagonal = diagonal + jnp.where(below, live, 0.0)
        pivot = diagonal if l == 0 else diagonal - face_z[l - 1] * up_gain[l - 1]
        inverse = 1.0 / pivot
        inv_pivot[l] = inverse
        if l > 0:
            down_gain[l] = face_z[l - 1] * inverse
        if l < depth - 1:
            up_gain[l] = face_z[l] * inverse
        here = slice(l, l + 1)
        joint = face_z[l] if l < depth - 1 else live
        edge_face[here] = face[width - 1 : width]
        for k, plane in enumerate((face_low, face_yu[l], inverse, joint)):
            coef_hi[k, here] = plane[width - 1 : width]
        for k, plane in enumerate((face, face_yu[l], inverse, joint)):
            coef_lo[k, here] = plane[0:1]

    store_sat = pltpu.make_async_copy(sat_res, sat_out, out_sem.at[0])
    store_sat.start()

    def moment(left, right):
        total = None
        for l in range(depth):
            term = left[l] * right[l]
            total = term if total is None else total + term
        return total

    def fold(plane):
        total = plane[:, 0:128]
        for start in range(128, span, 128):
            total = total + plane[:, start : start + 128]
        return jnp.sum(total, axis=0, keepdims=True)

    older = None
    current = [resid[l] for l in range(depth)]
    products = []
    for step in range(ITERS):
        partial = [current[0] * inv_pivot[0]]
        for l in range(1, depth):
            partial.append(current[l] * inv_pivot[l] + down_gain[l] * partial[l - 1])
        vector = [None] * depth
        vector[depth - 1] = partial[depth - 1]
        for l in range(depth - 2, -1, -1):
            vector[l] = partial[l] + up_gain[l] * vector[l + 1]
        wide = step % 2 == 0
        for l in range(depth):
            basis[step, l] = vector[l]
            if wide:
                here = slice(l, l + 1)
                vec_hi[step, 0, here] = vector[l][width - 1 : width]
                vec_hi[step, 1, here] = vector[l][width - 2 : width - 1]
                vec_lo[step, 0, here] = vector[l][0:1]
                vec_lo[step, 1, here] = vector[l][1:2]
        tag = 8 * step

        def hop(src, dst, target):
            nonlocal tag
            tag += 1
            return remote(src, dst, vec_send.at[tag - 1], vec_recv.at[tag - 1], target)

        ups, lows = [], []
        if wide:
            outer = basis[step, edge]
            diag_hi[step] = outer[width - 1 : width]
            diag_lo[step] = outer[0:1]
            ups = [
                hop(vec_hi.at[step], got_lo.at[step], upper_id),
                hop(diag_hi.at[step], got_diag_lo.at[step], upper_diag),
            ]
            lows = [
                hop(vec_lo.at[step], got_hi.at[step], lower_id),
                hop(diag_lo.at[step], got_diag_hi.at[step], lower_diag),
            ]
        trio = (ups, lows, [hop(basis.at[step, edge], got_z.at[step], other_id)])
        copies.append(trio)
        exchange(*trio)
        if step == 0:
            coefs = (
                [hop(coef_hi, got_coef_lo, upper_id)],
                [hop(coef_lo, got_coef_hi, lower_id)],
                [],
            )
            copies.append(coefs)
            exchange(*coefs)
        products.append(fold(moment(vector, current)))
        for l in range(depth):
            near = (
                face_xu[l] * next_x(vector[l])
                + face_xl[l] * prev_x(vector[l])
                + face_yu[l] * next_y(vector[l])
                + face_yl[l] * prev_y(vector[l])
            )
            source[l] = near
        arrived(*trio)
        source[edge] = source[edge] + face_zedge[...] * got_z[step]
        later = []
        for l in range(depth):
            halo = jnp.where(
                rows < width // 2, got_lo[step, 0, l : l + 1], got_hi[step, 0, l : l + 1]
            )
            value = source[l] + face_edge[l] * halo
            if step > 0:
                value = 2.0 * value - older[l]
            later.append(value)
        products.append(fold(moment(vector, later)))
        if wide:
            if step == 0:
                arrived(*coefs)
                halo_old = [None, None]
            sides = (
                (got_lo, vec_lo, got_coef_lo, got_diag_lo, recv_lo[3] * send_lo[3]),
                (got_hi, vec_hi, got_coef_hi, got_diag_hi, edge_face[...]),
            )
            for side, (got, own, coef, diag, between) in enumerate(sides):
                beside_it = got[step, 0]
                value = (
                    coef[0] * got[step, 1]
                    + between * own[step, 0]
                    + coef[1] * next_y(beside_it)
                    + prev_y(coef[1] * beside_it)
                )
                joint = coef[3, depth - 1 : depth]
                value = value + jnp.where(strip_rows == edge, joint * diag[step], 0.0)
                if step > 0:
                    value = 2.0 * value - halo_old[side]
                halo_old[side] = value
                inverse = coef[2]
                scaled_value = value * inverse
                gain_up = coef[3] * inverse
                part = [scaled_value[0:1]]
                for l in range(1, depth):
                    gain = coef[3, l - 1 : l] * inverse[l : l + 1]
                    part.append(scaled_value[l : l + 1] + gain * part[l - 1])
                solved = part[depth - 1]
                got[step + 1, 0, depth - 1 : depth] = solved
                for l in range(depth - 2, -1, -1):
                    solved = part[l] + gain_up[l : l + 1] * solved
                    got[step + 1, 0, l : l + 1] = solved
        older, current = current, later

    for k, value in enumerate(products):
        sums[0, k : k + 1] = value
    sends = []
    slot = 0
    for place_of, stage in enumerate(stages):
        batch = [
            remote(
                sums.at[place_of], others.at[slot + k],
                sum_send.at[slot + k], sum_recv.at[slot + k], peer_id,
            )
            for k, peer_id in enumerate(stage)
        ]
        for copy in batch:
            copy.start()
        total = sums[place_of]
        for k, copy in enumerate(batch):
            copy.wait_recv()
        for k in range(len(batch)):
            total = total + others[slot + k]
        if place_of + 1 < len(stages):
            sums[place_of + 1] = total
        sends += batch
        slot += len(batch)
    total = jnp.sum(total, axis=1, keepdims=True)
    raw = [total[k : k + 1] for k in range(2 * ITERS)]
    moments = [raw[0], raw[1]]
    for k in range(2, 2 * ITERS):
        moments.append(2.0 * raw[k] - raw[k % 2])
    weights = [jnp.broadcast_to(value, (width, span)) for value in galerkin(moments)]
    for l in range(depth):
        value = weights[0] * basis[0, l]
        for step in range(1, ITERS):
            value = value + weights[step] * basis[step, l]
        sol_res[l] = value
    store_sol = pltpu.make_async_copy(sol_res, sol_out, out_sem.at[1])
    store_sol.start()
    for trio in copies:
        departed(*trio)
    for copy in sends:
        copy.wait_send()
    store_sat.wait()
    store_sol.wait()


def hand_over(sat_in, sol_in, sat_out, sol_out, sem):
    moves = [
        pltpu.make_async_copy(sat_in, sat_out, sem.at[0]),
        pltpu.make_async_copy(sol_in, sol_out, sem.at[1]),
    ]
    for move in moves:
        move.start()
    for move in moves:
        move.wait()


def on_device(areal_count, *arrays):
    arrays = list(arrays)
    block = arrays[0].shape
    depth, width, span = block
    wells = arrays[7].shape[0]
    arrays[7] = arrays[7].reshape(1, wells)
    arrays[8] = arrays[8].reshape(1, wells)
    plane = (width, span)
    strip = (depth, span)
    low = min(LOW_GROUP, areal_count)
    slots = low + (areal_count // low - 1)
    f32 = jnp.float32
    cube = pltpu.VMEM(block, f32)

    def vmem(*shape):
        return pltpu.VMEM(shape, f32)

    scratch = [
        cube, cube, cube, cube, cube, vmem(3, *block), pltpu.VMEM(block, jnp.int32),
        pltpu.VMEM((1, wells), jnp.int32), vmem(1, wells),
        cube, cube, cube, cube, cube, cube,
        cube, cube, cube, cube,
        cube, cube, cube, cube, cube, vmem(*plane),
        vmem(ITERS, *block), cube,
        vmem(5, *strip), vmem(4, *strip), vmem(6, *plane),
        vmem(4, *strip), vmem(5, *strip), vmem(6, *plane),
        vmem(ITERS, 2, *strip), vmem(ITERS, 2, *strip),
        vmem(ITERS, 2, *strip), vmem(ITERS, 2, *strip), vmem(ITERS, *plane),
        vmem(4, *strip), vmem(4, *strip), vmem(4, *strip), vmem(4, *strip), vmem(*strip),
        vmem(ITERS, 1, span), vmem(ITERS, 1, span), vmem(ITERS, 1, span), vmem(ITERS, 1, span),
        vmem(3, 2 * ITERS, 128), vmem(slots, 2 * ITERS, 128),
        pltpu.SemaphoreType.DMA((9,)), pltpu.SemaphoreType.DMA((2,)),
        pltpu.SemaphoreType.DMA((3,)), pltpu.SemaphoreType.DMA((3,)),
        pltpu.SemaphoreType.DMA((8 * ITERS,)), pltpu.SemaphoreType.DMA((8 * ITERS,)),
        pltpu.SemaphoreType.DMA((slots,)), pltpu.SemaphoreType.DMA((slots,)),
    ]
    results = pl.pallas_call(
        functools.partial(kernel, areal_count),
        out_shape=(jax.ShapeDtypeStruct(block, f32), jax.ShapeDtypeStruct(block, f32)),
        in_specs=[pl.BlockSpec(memory_space=pl.ANY)] * len(arrays),
        out_specs=(pl.BlockSpec(memory_space=pl.ANY), pl.BlockSpec(memory_space=pl.ANY)),
        scratch_shapes=scratch,
        compiler_params=pltpu.CompilerParams(
            collective_id=0, has_side_effects=True, vmem_limit_bytes=60 * 1024 * 1024
        ),
    )(*arrays)
    return pl.pallas_call(
        hand_over,
        out_shape=(jax.ShapeDtypeStruct(block, f32), jax.ShapeDtypeStruct(block, f32)),
        in_specs=[pl.BlockSpec(memory_space=pl.ANY)] * 2,
        out_specs=(pl.BlockSpec(memory_space=pl.ANY), pl.BlockSpec(memory_space=pl.ANY)),
        scratch_shapes=[pltpu.SemaphoreType.DMA((2,))],
    )(*results)


def solution(mesh):
    block = P(("members", "layer"), "areal", None)
    return jax.shard_map(
        functools.partial(on_device, mesh.shape["areal"]),
        mesh=mesh,
        in_specs=(
            block, block, block, block, block,
            P(None, ("members", "layer"), "areal", None),
            block, P("members"), P("members"),
        ),
        out_specs=(block, block),
        check_vma=False,
    )
```

```python
import functools

import jax
import jax.numpy as jnp
from jax import lax
from jax.experimental import pallas as pl
from jax.experimental.pallas import tpu as pltpu
from jax.sharding import PartitionSpec as P

ITERS = 4
MOBILITY_RATIO = 0.5
LOW_GROUP = 8
MESH = pl.DeviceIdType.MESH


def flow_fraction(wetness):
    square = wetness * wetness
    dry = 1.0 - wetness
    inverse = 1.0 / (square + MOBILITY_RATIO * (dry * dry))
    return square * inverse, (2.0 * MOBILITY_RATIO) * wetness * dry * (inverse * inverse)


def face_terms(face, scaled, press, frac, slope, upwind):
    moved = face * (scaled[1] - scaled[0])
    push = moved * jnp.where(upwind, frac[0], frac[1])
    drive = moved * (press[0] - press[1]) * jnp.where(upwind, slope[0], slope[1])
    return push, jnp.where(upwind, drive, 0.0), jnp.where(upwind, 0.0, drive)


def galerkin(moments):
    def inner(i, j):
        return 0.5 * (moments[i + j] + moments[abs(i - j)])

    def entry(i, j):
        moved = inner(i, 1) if j == 0 else 0.5 * (inner(i, j + 1) + inner(i, j - 1))
        return inner(i, j) - moved

    size = ITERS
    lower = [[None] * size for _ in range(size)]
    inverse = []
    forward = []
    for i in range(size):
        for j in range(i):
            total = entry(i, j)
            for k in range(j):
                total = total - lower[i][k] * lower[j][k] * inverse[k]
            lower[i][j] = total
        diagonal = entry(i, i)
        pivot = diagonal
        right = moments[i]
        for k in range(i):
            scale = lower[i][k] * inverse[k]
            pivot = pivot - scale * lower[i][k]
            right = right - scale * forward[k]
        keep = pivot > 1e-6 * diagonal
        inv = jnp.where(keep, 1.0 / jnp.where(keep, pivot, 1.0), 0.0)
        inverse.append(inv)
        forward.append(right)
    solved = [None] * size
    for i in range(size - 1, -1, -1):
        total = forward[i]
        for k in range(i + 1, size):
            total = total - lower[k][i] * solved[k]
        solved[i] = total * inverse[i]
    return solved


def kernel(
    areal_count,
    press_in, wet_in, cot_in, dt_in, comp_in, trans_in, flags_in, cells_in, misfit_in,
    sat_out, sol_out,
    press, wet, cot, dt, comp, trans, flags, cells, misfit,
    scaled, frac, slope, resid, sat_res, sol_res,
    face_z, inv_pivot, down_gain, up_gain,
    face_xu, face_xl, face_yu, face_yl, face_edge, face_zedge,
    basis, source,
    send_hi, send_lo, send_z, recv_hi, recv_lo, recv_z,
    vec_hi, vec_lo, got_hi, got_lo, got_z,
    coef_hi, coef_lo, got_coef_hi, got_coef_lo, edge_face,
    diag_hi, diag_lo, got_diag_hi, got_diag_lo,
    sums, others,
    in_sem, out_sem, face_send, face_recv, vec_send, vec_recv, sum_send, sum_recv,
):
    depth, width, span = press.shape
    areal = lax.axis_index("areal")
    layer = lax.axis_index("layer")
    has_lo = areal > 0
    has_hi = areal < areal_count - 1
    lower_id = {"areal": jnp.maximum(areal - 1, 0), "layer": layer}
    upper_id = {"areal": jnp.minimum(areal + 1, areal_count - 1), "layer": layer}
    other_id = {"areal": areal, "layer": 1 - layer}
    lower_diag = {"areal": jnp.maximum(areal - 1, 0), "layer": 1 - layer}
    upper_diag = {"areal": jnp.minimum(areal + 1, areal_count - 1), "layer": 1 - layer}
    edge = (depth - 1) * (1 - layer)

    low = min(LOW_GROUP, areal_count)
    high = areal_count // low
    place = lax.rem(areal, low)
    first = areal - place
    stages = [
        [other_id],
        [
            {"areal": first + lax.rem(place + step, low), "layer": layer}
            for step in range(1, low)
        ],
    ]
    if high > 1:
        row = lax.div(areal, low)
        stages.append(
            [
                {"areal": lax.rem(row + step, high) * low + place, "layer": layer}
                for step in range(1, high)
            ]
        )

    pairs = [
        (cells_in, cells), (misfit_in, misfit), (cot_in, cot), (dt_in, dt), (flags_in, flags),
        (press_in, press), (wet_in, wet), (trans_in, trans), (comp_in, comp),
    ]
    loads = [
        pltpu.make_async_copy(src, dst, in_sem.at[place_of])
        for place_of, (src, dst) in enumerate(pairs)
    ]
    for load in loads:
        load.start()

    barrier = pltpu.get_barrier_semaphore()
    for stage in stages:
        for peer_id in stage:
            pl.semaphore_signal(barrier, inc=1, device_id=peer_id, device_id_type=MESH)
    expected = sum(len(stage) for stage in stages)
    beside = 2 if high > 1 else 1

    @pl.when(has_lo)
    def _():
        for peer_id in (lower_diag, lower_id)[:beside]:
            pl.semaphore_signal(barrier, inc=1, device_id=peer_id, device_id_type=MESH)

    @pl.when(has_hi)
    def _():
        for peer_id in (upper_diag, upper_id)[:beside]:
            pl.semaphore_signal(barrier, inc=1, device_id=peer_id, device_id_type=MESH)

    @pl.when(jnp.logical_not(has_lo))
    def _():
        recv_lo[...] = jnp.zeros_like(recv_lo)
        got_lo[...] = jnp.zeros_like(got_lo)
        got_coef_lo[...] = jnp.zeros_like(got_coef_lo)
        got_diag_lo[...] = jnp.zeros_like(got_diag_lo)

    @pl.when(jnp.logical_not(has_hi))
    def _():
        recv_hi[...] = jnp.zeros_like(recv_hi)
        got_hi[...] = jnp.zeros_like(got_hi)
        got_coef_hi[...] = jnp.zeros_like(got_coef_hi)
        got_diag_hi[...] = jnp.zeros_like(got_diag_hi)

    rows = lax.broadcasted_iota(jnp.int32, (width, span), 0)
    lanes = lax.broadcasted_iota(jnp.int32, (width, span), 1)
    is_low_row = rows == 0
    is_high_row = rows == width - 1
    is_last_lane = lanes == span - 1
    strip_rows = lax.broadcasted_iota(jnp.int32, (depth, span), 0)

    def next_y(value):
        return pltpu.roll(value, span - 1, 1)

    def prev_y(value):
        return pltpu.roll(value, 1, 1)

    def next_x(value):
        return pltpu.roll(value, width - 1, 0)

    def prev_x(value):
        return pltpu.roll(value, 1, 0)

    loads[0].wait()
    loads[1].wait()
    cell = cells[...]
    wells = cell.shape[1]
    local = lax.broadcasted_iota(jnp.int32, (depth * width, wells), 0)
    base = (
        (layer * depth + lax.shift_right_logical(local, (width - 1).bit_length()))
        * (areal_count * width)
        + areal * width + lax.bitwise_and(local, width - 1)
    ) * span
    offset = cell - base
    by_row = jnp.where((offset >= 0) & (offset < span), misfit[...], 0.0)
    lane_of = lax.bitwise_and(cell, span - 1)
    by_lane = jnp.where(
        lax.broadcasted_iota(jnp.int32, (span, wells), 0) == lane_of, 1.0, 0.0
    )
    added = lax.dot_general(
        by_row, by_lane, (((1,), (1,)), ((), ())),
        precision=lax.Precision.HIGHEST, preferred_element_type=jnp.float32,
    )
    for load in loads[2:8]:
        load.wait()
    act = []
    for l in range(depth):
        modified = cot[l] + added[l * width : (l + 1) * width]
        sat_res[l] = modified
        scaled[l] = dt[l] * modified
        act.append(jnp.where((flags[l] & 8) != 0, 1.0, 0.0))

    for l in range(depth):
        here = slice(l, l + 1)
        top = slice(width - 1, width)
        live_x = trans[1, l] * act[l]
        up_x = jnp.where((flags[l] & 2) != 0, 1.0, 0.0)
        for k, plane in enumerate((press[l], scaled[l], wet[l], live_x, up_x)):
            send_hi[k, here] = plane[top]
        for k, plane in enumerate((press[l], scaled[l], wet[l], act[l])):
            send_lo[k, here] = plane[0:1]
    edge_act = jnp.where((flags[edge] & 8) != 0, 1.0, 0.0)
    send_z[0] = press[edge]
    send_z[1] = scaled[edge]
    send_z[2] = wet[edge]
    send_z[3] = edge_act
    send_z[4] = trans[0, edge] * edge_act
    send_z[5] = jnp.where((flags[edge] & 1) != 0, 1.0, 0.0)

    sides_there = jnp.where(has_lo, 1, 0) + jnp.where(has_hi, 1, 0)
    pl.semaphore_wait(barrier, expected + beside * sides_there)

    def remote(src, dst, send_sem, recv_sem, target):
        return pltpu.make_async_remote_copy(
            src_ref=src, dst_ref=dst, send_sem=send_sem, recv_sem=recv_sem,
            device_id=target, device_id_type=MESH,
        )

    def exchange(ups, lows, across):
        if ups:
            @pl.when(has_hi)
            def _():
                for copy in ups:
                    copy.start()

            @pl.when(has_lo)
            def _():
                for copy in lows:
                    copy.start()

        for copy in across:
            copy.start()

    def arrived(ups, lows, across):
        for copy in across:
            copy.wait_recv()
        if ups:
            @pl.when(has_lo)
            def _():
                for copy in ups:
                    copy.wait_recv()

            @pl.when(has_hi)
            def _():
                for copy in lows:
                    copy.wait_recv()

    def departed(ups, lows, across):
        for copy in across:
            copy.wait_send()
        if ups:
            @pl.when(has_hi)
            def _():
                for copy in ups:
                    copy.wait_send()

            @pl.when(has_lo)
            def _():
                for copy in lows:
                    copy.wait_send()

    copies = [
        (
            [remote(send_hi, recv_lo, face_send.at[0], face_recv.at[0], upper_id)],
            [remote(send_lo, recv_hi, face_send.at[1], face_recv.at[1], lower_id)],
            [remote(send_z, recv_z, face_send.at[2], face_recv.at[2], other_id)],
        )
    ]
    exchange(*copies[0])

    for l in range(depth):
        share, rise = flow_fraction(wet[l])
        frac[l] = share
        slope[l] = rise
    carried = None
    for l in range(depth):
        up = (flags[l] & 4) != 0
        face = jnp.where(is_last_lane, 0.0, trans[2, l] * act[l] * next_y(act[l]))
        face_yu[l] = face
        face_yl[l] = prev_y(face)
        push, drive_here, drive_next = face_terms(
            face,
            (scaled[l], next_y(scaled[l])),
            (press[l], next_y(press[l])),
            (frac[l], next_y(frac[l])),
            (slope[l], next_y(slope[l])),
            up,
        )
        pushed = push - prev_y(push)
        driven = sat_res[l] + drive_here + prev_y(drive_next)
        if carried is not None:
            pushed = pushed - carried[0]
            driven = driven + carried[1]
        if l < depth - 1:
            face = trans[0, l] * act[l] * act[l + 1]
            face_z[l] = face
            push, drive_here, drive_next = face_terms(
                face,
                (scaled[l], scaled[l + 1]),
                (press[l], press[l + 1]),
                (frac[l], frac[l + 1]),
                (slope[l], slope[l + 1]),
                (flags[l] & 1) != 0,
            )
            pushed = pushed + push
            driven = driven + drive_here
            carried = (push, drive_next)
        resid[l] = pushed
        sat_res[l] = driven

    arrived(*copies[0])

    below = layer == 0
    z_share, z_rise = flow_fraction(recv_z[2])
    live = jnp.where(below, trans[0, edge] * edge_act * recv_z[3], recv_z[4] * edge_act)
    face_zedge[...] = live
    up_edge = jnp.where(below, send_z[5], recv_z[5]) > 0.5

    def ordered(mine, theirs):
        return jnp.where(below, mine, theirs), jnp.where(below, theirs, mine)

    push, drive_here, drive_next = face_terms(
        live,
        ordered(send_z[1], recv_z[1]),
        ordered(send_z[0], recv_z[0]),
        ordered(frac[edge], z_share),
        ordered(slope[edge], z_rise),
        up_edge,
    )
    resid[edge] = resid[edge] + jnp.where(below, push, -push)
    sat_res[edge] = sat_res[edge] + jnp.where(below, drive_here, drive_next)

    hi_share, hi_rise = flow_fraction(recv_hi[2])
    lo_share, lo_rise = flow_fraction(recv_lo[2])
    own_share, own_rise = flow_fraction(send_lo[2])
    low_face = recv_lo[3] * send_lo[3]
    low_push, _, low_drive = face_terms(
        low_face,
        (recv_lo[1], send_lo[1]),
        (recv_lo[0], send_lo[0]),
        (lo_share, own_share),
        (lo_rise, own_rise),
        recv_lo[4] > 0.5,
    )
    hi_press, hi_scaled, hi_act = recv_hi[0], recv_hi[1], recv_hi[3]

    def with_high(value, plane, l):
        return jnp.where(is_high_row, plane[l : l + 1], next_x(value))

    def with_low(value, plane, l):
        return jnp.where(is_low_row, plane[l : l + 1], prev_x(value))

    loads[8].wait()
    for l in range(depth):
        face = trans[1, l] * act[l] * with_high(act[l], hi_act, l)
        push, drive_here, drive_next = face_terms(
            face,
            (scaled[l], with_high(scaled[l], hi_scaled, l)),
            (press[l], with_high(press[l], hi_press, l)),
            (frac[l], with_high(frac[l], hi_share, l)),
            (slope[l], with_high(slope[l], hi_rise, l)),
            (flags[l] & 2) != 0,
        )
        resid[l] = resid[l] + push - with_low(push, low_push, l)
        sat_res[l] = sat_res[l] + drive_here + with_low(drive_next, low_drive, l)
        face_low = with_low(face, low_face, l)
        face_xu[l] = jnp.where(is_high_row, 0.0, face)
        face_xl[l] = jnp.where(is_low_row, 0.0, face_low)
        face_edge[l] = jnp.where(
            is_high_row, face, jnp.where(is_low_row, face_low, 0.0)
        )
        diagonal = comp[l] + face + face_low + face_yu[l] + face_yl[l]
        if l > 0:
            diagonal = diagonal + face_z[l - 1]
        else:
            diagonal = diagonal + jnp.where(below, 0.0, live)
        if l < depth - 1:
            diagonal = diagonal + face_z[l]
        else:
            diagonal = diagonal + jnp.where(below, live, 0.0)
        pivot = diagonal if l == 0 else diagonal - face_z[l - 1] * up_gain[l - 1]
        inverse = 1.0 / pivot
        inv_pivot[l] = inverse
        if l > 0:
            down_gain[l] = face_z[l - 1] * inverse
        if l < depth - 1:
            up_gain[l] = face_z[l] * inverse
        here = slice(l, l + 1)
        joint = face_z[l] if l < depth - 1 else live
        edge_face[here] = face[width - 1 : width]
        for k, plane in enumerate((face_low, face_yu[l], inverse, joint)):
            coef_hi[k, here] = plane[width - 1 : width]
        for k, plane in enumerate((face, face_yu[l], inverse, joint)):
            coef_lo[k, here] = plane[0:1]

    store_sat = pltpu.make_async_copy(sat_res, sat_out, out_sem.at[0])
    store_sat.start()

    def moment(left, right):
        total = None
        for l in range(depth):
            term = left[l] * right[l]
            total = term if total is None else total + term
        return total

    def fold(plane):
        total = plane[:, 0:128]
        for start in range(128, span, 128):
            total = total + plane[:, start : start + 128]
        return jnp.sum(total, axis=0, keepdims=True)

    halo_old = [None, None]

    def advance_halo(step):
            if step == 0:
                arrived(*coefs)
            sides = (
                (got_lo, vec_lo, got_coef_lo, got_diag_lo, recv_lo[3] * send_lo[3]),
                (got_hi, vec_hi, got_coef_hi, got_diag_hi, edge_face[...]),
            )
            for side, (got, own, coef, diag, between) in enumerate(sides):
                beside_it = got[step, 0]
                value = (
                    coef[0] * got[step, 1]
                    + between * own[step, 0]
                    + coef[1] * next_y(beside_it)
                    + prev_y(coef[1] * beside_it)
                )
                joint = coef[3, depth - 1 : depth]
                value = value + jnp.where(strip_rows == edge, joint * diag[step], 0.0)
                if step > 0:
                    value = 2.0 * value - halo_old[side]
                halo_old[side] = value
                inverse = coef[2]
                scaled_value = value * inverse
                gain_up = coef[3] * inverse
                part = [scaled_value[0:1]]
                for l in range(1, depth):
                    gain = coef[3, l - 1 : l] * inverse[l : l + 1]
                    part.append(scaled_value[l : l + 1] + gain * part[l - 1])
                solved = part[depth - 1]
                got[step + 1, 0, depth - 1 : depth] = solved
                for l in range(depth - 2, -1, -1):
                    solved = part[l] + gain_up[l : l + 1] * solved
                    got[step + 1, 0, l : l + 1] = solved

    older = None
    current = [resid[l] for l in range(depth)]
    products = []
    for step in range(ITERS):
        partial = [current[0] * inv_pivot[0]]
        for l in range(1, depth):
            partial.append(current[l] * inv_pivot[l] + down_gain[l] * partial[l - 1])
        vector = [None] * depth
        vector[depth - 1] = partial[depth - 1]
        for l in range(depth - 2, -1, -1):
            vector[l] = partial[l] + up_gain[l] * vector[l + 1]
        wide = step % 2 == 0
        for l in range(depth):
            basis[step, l] = vector[l]
            if wide:
                here = slice(l, l + 1)
                vec_hi[step, 0, here] = vector[l][width - 1 : width]
                vec_hi[step, 1, here] = vector[l][width - 2 : width - 1]
                vec_lo[step, 0, here] = vector[l][0:1]
                vec_lo[step, 1, here] = vector[l][1:2]
        tag = 8 * step

        def hop(src, dst, target):
            nonlocal tag
            tag += 1
            return remote(src, dst, vec_send.at[tag - 1], vec_recv.at[tag - 1], target)

        ups, lows = [], []
        if wide:
            outer = basis[step, edge]
            diag_hi[step] = outer[width - 1 : width]
            diag_lo[step] = outer[0:1]
            ups = [
                hop(vec_hi.at[step], got_lo.at[step], upper_id),
                hop(diag_hi.at[step], got_diag_lo.at[step], upper_diag),
            ]
            lows = [
                hop(vec_lo.at[step], got_hi.at[step], lower_id),
                hop(diag_lo.at[step], got_diag_hi.at[step], lower_diag),
            ]
        trio = (ups, lows, [hop(basis.at[step, edge], got_z.at[step], other_id)])
        copies.append(trio)
        exchange(*trio)
        if step == 0:
            coefs = (
                [hop(coef_hi, got_coef_lo, upper_id)],
                [hop(coef_lo, got_coef_hi, lower_id)],
                [],
            )
            copies.append(coefs)
            exchange(*coefs)
        products.append(fold(moment(vector, current)))
        for l in range(depth):
            near = (
                face_xu[l] * next_x(vector[l])
                + face_xl[l] * prev_x(vector[l])
                + face_yu[l] * next_y(vector[l])
                + face_yl[l] * prev_y(vector[l])
            )
            source[l] = near
        arrived(*trio)
        if not wide:
            advance_halo(step - 1)
        source[edge] = source[edge] + face_zedge[...] * got_z[step]
        later = []
        for l in range(depth):
            halo = jnp.where(
                rows < width // 2, got_lo[step, 0, l : l + 1], got_hi[step, 0, l : l + 1]
            )
            value = source[l] + face_edge[l] * halo
            if step > 0:
                value = 2.0 * value - older[l]
            later.append(value)
        products.append(fold(moment(vector, later)))
        older, current = current, later

    for k, value in enumerate(products):
        sums[0, k : k + 1] = value
    sends = []
    slot = 0
    for place_of, stage in enumerate(stages):
        batch = [
            remote(
                sums.at[place_of], others.at[slot + k],
                sum_send.at[slot + k], sum_recv.at[slot + k], peer_id,
            )
            for k, peer_id in enumerate(stage)
        ]
        for copy in batch:
            copy.start()
        total = sums[place_of]
        for k, copy in enumerate(batch):
            copy.wait_recv()
        for k in range(len(batch)):
            total = total + others[slot + k]
        if place_of + 1 < len(stages):
            sums[place_of + 1] = total
        sends += batch
        slot += len(batch)
    total = jnp.sum(total, axis=1, keepdims=True)
    raw = [total[k : k + 1] for k in range(2 * ITERS)]
    moments = [raw[0], raw[1]]
    for k in range(2, 2 * ITERS):
        moments.append(2.0 * raw[k] - raw[k % 2])
    weights = [jnp.broadcast_to(value, (width, span)) for value in galerkin(moments)]
    for l in range(depth):
        value = weights[0] * basis[0, l]
        for step in range(1, ITERS):
            value = value + weights[step] * basis[step, l]
        sol_res[l] = value
    store_sol = pltpu.make_async_copy(sol_res, sol_out, out_sem.at[1])
    store_sol.start()
    for trio in copies:
        departed(*trio)
    for copy in sends:
        copy.wait_send()
    store_sat.wait()
    store_sol.wait()


def on_device(areal_count, *arrays):
    arrays = list(arrays)
    block = arrays[0].shape
    depth, width, span = block
    wells = arrays[7].shape[0]
    arrays[7] = arrays[7].reshape(1, wells)
    arrays[8] = arrays[8].reshape(1, wells)
    plane = (width, span)
    strip = (depth, span)
    low = min(LOW_GROUP, areal_count)
    slots = low + (areal_count // low - 1)
    f32 = jnp.float32
    cube = pltpu.VMEM(block, f32)

    def vmem(*shape):
        return pltpu.VMEM(shape, f32)

    scratch = [
        cube, cube, cube, cube, cube, vmem(3, *block), pltpu.VMEM(block, jnp.int32),
        pltpu.VMEM((1, wells), jnp.int32), vmem(1, wells),
        cube, cube, cube, cube, cube, cube,
        cube, cube, cube, cube,
        cube, cube, cube, cube, cube, vmem(*plane),
        vmem(ITERS, *block), cube,
        vmem(5, *strip), vmem(4, *strip), vmem(6, *plane),
        vmem(4, *strip), vmem(5, *strip), vmem(6, *plane),
        vmem(ITERS, 2, *strip), vmem(ITERS, 2, *strip),
        vmem(ITERS, 2, *strip), vmem(ITERS, 2, *strip), vmem(ITERS, *plane),
        vmem(4, *strip), vmem(4, *strip), vmem(4, *strip), vmem(4, *strip), vmem(*strip),
        vmem(ITERS, 1, span), vmem(ITERS, 1, span), vmem(ITERS, 1, span), vmem(ITERS, 1, span),
        vmem(3, 2 * ITERS, 128), vmem(slots, 2 * ITERS, 128),
        pltpu.SemaphoreType.DMA((9,)), pltpu.SemaphoreType.DMA((2,)),
        pltpu.SemaphoreType.DMA((3,)), pltpu.SemaphoreType.DMA((3,)),
        pltpu.SemaphoreType.DMA((8 * ITERS,)), pltpu.SemaphoreType.DMA((8 * ITERS,)),
        pltpu.SemaphoreType.DMA((slots,)), pltpu.SemaphoreType.DMA((slots,)),
    ]
    return pl.pallas_call(
        functools.partial(kernel, areal_count),
        out_shape=(jax.ShapeDtypeStruct(block, f32), jax.ShapeDtypeStruct(block, f32)),
        in_specs=[pl.BlockSpec(memory_space=pl.ANY)] * len(arrays),
        out_specs=(pl.BlockSpec(memory_space=pl.ANY), pl.BlockSpec(memory_space=pl.ANY)),
        scratch_shapes=scratch,
        compiler_params=pltpu.CompilerParams(
            collective_id=0, has_side_effects=True, vmem_limit_bytes=60 * 1024 * 1024
        ),
    )(*arrays)


def solution(mesh):
    block = P(("members", "layer"), "areal", None)
    return jax.shard_map(
        functools.partial(on_device, mesh.shape["areal"]),
        mesh=mesh,
        in_specs=(
            block, block, block, block, block,
            P(None, ("members", "layer"), "areal", None),
            block, P("members"), P("members"),
        ),
        out_specs=(block, block),
        check_vma=False,
    )
```

```python
import functools

import jax
import jax.numpy as jnp
from jax import lax
from jax.experimental import pallas as pl
from jax.experimental.pallas import tpu as pltpu
from jax.sharding import PartitionSpec as P

ITERS = 4
MOBILITY_RATIO = 0.5
LOW_GROUP = 8
MESH = pl.DeviceIdType.MESH


def flow_fraction(wetness):
    square = wetness * wetness
    dry = 1.0 - wetness
    inverse = 1.0 / (square + MOBILITY_RATIO * (dry * dry))
    return square * inverse, (2.0 * MOBILITY_RATIO) * wetness * dry * (inverse * inverse)


def face_terms(face, scaled, press, frac, slope, upwind):
    moved = face * (scaled[1] - scaled[0])
    push = moved * jnp.where(upwind, frac[0], frac[1])
    drive = moved * (press[0] - press[1]) * jnp.where(upwind, slope[0], slope[1])
    return push, jnp.where(upwind, drive, 0.0), jnp.where(upwind, 0.0, drive)


def galerkin(moments):
    def inner(i, j):
        return 0.5 * (moments[i + j] + moments[abs(i - j)])

    def entry(i, j):
        moved = inner(i, 1) if j == 0 else 0.5 * (inner(i, j + 1) + inner(i, j - 1))
        return inner(i, j) - moved

    size = ITERS
    lower = [[None] * size for _ in range(size)]
    inverse = []
    forward = []
    for i in range(size):
        for j in range(i):
            total = entry(i, j)
            for k in range(j):
                total = total - lower[i][k] * lower[j][k] * inverse[k]
            lower[i][j] = total
        diagonal = entry(i, i)
        pivot = diagonal
        right = moments[i]
        for k in range(i):
            scale = lower[i][k] * inverse[k]
            pivot = pivot - scale * lower[i][k]
            right = right - scale * forward[k]
        keep = pivot > 1e-6 * diagonal
        inv = jnp.where(keep, 1.0 / jnp.where(keep, pivot, 1.0), 0.0)
        inverse.append(inv)
        forward.append(right)
    solved = [None] * size
    for i in range(size - 1, -1, -1):
        total = forward[i]
        for k in range(i + 1, size):
            total = total - lower[k][i] * solved[k]
        solved[i] = total * inverse[i]
    return solved


def kernel(
    areal_count,
    press_in, wet_in, cot_in, dt_in, comp_in, trans_in, flags_in, cells_in, misfit_in,
    sat_out, sol_out,
    press, wet, cot, dt, comp, trans, flags, cells, misfit,
    scaled, frac, slope, resid, sat_res, sol_res,
    face_z, inv_pivot, down_gain, up_gain,
    face_xu, face_xl, face_yu, face_yl, face_edge, face_zedge,
    basis, source,
    send_hi, send_lo, send_z, recv_hi, recv_lo, recv_z,
    vec_hi, vec_lo, got_hi, got_lo, got_z,
    coef_hi, coef_lo, got_coef_hi, got_coef_lo, edge_face,
    diag_hi, diag_lo, got_diag_hi, got_diag_lo,
    sums, others,
    in_sem, out_sem, face_send, face_recv, vec_send, vec_recv, sum_send, sum_recv,
):
    depth, width, span = press.shape
    areal = lax.axis_index("areal")
    layer = lax.axis_index("layer")
    has_lo = areal > 0
    has_hi = areal < areal_count - 1
    lower_id = {"areal": jnp.maximum(areal - 1, 0), "layer": layer}
    upper_id = {"areal": jnp.minimum(areal + 1, areal_count - 1), "layer": layer}
    other_id = {"areal": areal, "layer": 1 - layer}
    lower_diag = {"areal": jnp.maximum(areal - 1, 0), "layer": 1 - layer}
    upper_diag = {"areal": jnp.minimum(areal + 1, areal_count - 1), "layer": 1 - layer}
    edge = (depth - 1) * (1 - layer)

    low = min(LOW_GROUP, areal_count)
    high = areal_count // low
    place = lax.rem(areal, low)
    first = areal - place
    stages = [
        [other_id],
        [
            {"areal": first + lax.rem(place + step, low), "layer": layer}
            for step in range(1, low)
        ],
    ]
    if high > 1:
        row = lax.div(areal, low)
        stages.append(
            [
                {"areal": lax.rem(row + step, high) * low + place, "layer": layer}
                for step in range(1, high)
            ]
        )

    pairs = [
        (cells_in, cells), (misfit_in, misfit), (cot_in, cot), (dt_in, dt), (flags_in, flags),
        (press_in, press), (wet_in, wet), (trans_in, trans), (comp_in, comp),
    ]
    loads = [
        pltpu.make_async_copy(src, dst, in_sem.at[place_of])
        for place_of, (src, dst) in enumerate(pairs)
    ]
    for load in loads:
        load.start()

    barrier = pltpu.get_barrier_semaphore()
    for stage in stages:
        for peer_id in stage:
            pl.semaphore_signal(barrier, inc=1, device_id=peer_id, device_id_type=MESH)
    expected = sum(len(stage) for stage in stages)
    beside = 2 if high > 1 else 1

    @pl.when(has_lo)
    def _():
        for peer_id in (lower_diag, lower_id)[:beside]:
            pl.semaphore_signal(barrier, inc=1, device_id=peer_id, device_id_type=MESH)

    @pl.when(has_hi)
    def _():
        for peer_id in (upper_diag, upper_id)[:beside]:
            pl.semaphore_signal(barrier, inc=1, device_id=peer_id, device_id_type=MESH)

    @pl.when(jnp.logical_not(has_lo))
    def _():
        recv_lo[...] = jnp.zeros_like(recv_lo)
        got_lo[...] = jnp.zeros_like(got_lo)
        got_coef_lo[...] = jnp.zeros_like(got_coef_lo)
        got_diag_lo[...] = jnp.zeros_like(got_diag_lo)

    @pl.when(jnp.logical_not(has_hi))
    def _():
        recv_hi[...] = jnp.zeros_like(recv_hi)
        got_hi[...] = jnp.zeros_like(got_hi)
        got_coef_hi[...] = jnp.zeros_like(got_coef_hi)
        got_diag_hi[...] = jnp.zeros_like(got_diag_hi)

    rows = lax.broadcasted_iota(jnp.int32, (width, span), 0)
    lanes = lax.broadcasted_iota(jnp.int32, (width, span), 1)
    is_low_row = rows == 0
    is_high_row = rows == width - 1
    is_last_lane = lanes == span - 1
    strip_rows = lax.broadcasted_iota(jnp.int32, (depth, span), 0)

    def next_y(value):
        return pltpu.roll(value, span - 1, 1)

    def prev_y(value):
        return pltpu.roll(value, 1, 1)

    def next_x(value):
        return pltpu.roll(value, width - 1, 0)

    def prev_x(value):
        return pltpu.roll(value, 1, 0)

    loads[0].wait()
    loads[1].wait()
    cell = cells[...]
    wells = cell.shape[1]
    local = lax.broadcasted_iota(jnp.int32, (depth * width, wells), 0)
    base = (
        (layer * depth + lax.shift_right_logical(local, (width - 1).bit_length()))
        * (areal_count * width)
        + areal * width + lax.bitwise_and(local, width - 1)
    ) * span
    offset = cell - base
    by_row = jnp.where((offset >= 0) & (offset < span), misfit[...], 0.0)
    lane_of = lax.bitwise_and(cell, span - 1)
    by_lane = jnp.where(
        lax.broadcasted_iota(jnp.int32, (span, wells), 0) == lane_of, 1.0, 0.0
    )
    added = lax.dot_general(
        by_row, by_lane, (((1,), (1,)), ((), ())),
        precision=lax.Precision.HIGHEST, preferred_element_type=jnp.float32,
    )
    for load in loads[2:8]:
        load.wait()
    act = []
    for l in range(depth):
        modified = cot[l] + added[l * width : (l + 1) * width]
        sat_res[l] = modified
        scaled[l] = dt[l] * modified
        act.append(jnp.where((flags[l] & 8) != 0, 1.0, 0.0))

    for l in range(depth):
        here = slice(l, l + 1)
        top = slice(width - 1, width)
        live_x = trans[1, l] * act[l]
        up_x = jnp.where((flags[l] & 2) != 0, 1.0, 0.0)
        for k, plane in enumerate((press[l], scaled[l], wet[l], live_x, up_x)):
            send_hi[k, here] = plane[top]
        for k, plane in enumerate((press[l], scaled[l], wet[l], act[l])):
            send_lo[k, here] = plane[0:1]
    edge_act = jnp.where((flags[edge] & 8) != 0, 1.0, 0.0)
    send_z[0] = press[edge]
    send_z[1] = scaled[edge]
    send_z[2] = wet[edge]
    send_z[3] = edge_act
    send_z[4] = trans[0, edge] * edge_act
    send_z[5] = jnp.where((flags[edge] & 1) != 0, 1.0, 0.0)

    sides_there = jnp.where(has_lo, 1, 0) + jnp.where(has_hi, 1, 0)
    pl.semaphore_wait(barrier, expected + beside * sides_there)

    def remote(src, dst, send_sem, recv_sem, target):
        return pltpu.make_async_remote_copy(
            src_ref=src, dst_ref=dst, send_sem=send_sem, recv_sem=recv_sem,
            device_id=target, device_id_type=MESH,
        )

    def exchange(ups, lows, across):
        if ups:
            @pl.when(has_hi)
            def _():
                for copy in ups:
                    copy.start()

            @pl.when(has_lo)
            def _():
                for copy in lows:
                    copy.start()

        for copy in across:
            copy.start()

    def arrived(ups, lows, across):
        for copy in across:
            copy.wait_recv()
        if ups:
            @pl.when(has_lo)
            def _():
                for copy in ups:
                    copy.wait_recv()

            @pl.when(has_hi)
            def _():
                for copy in lows:
                    copy.wait_recv()

    def departed(ups, lows, across):
        for copy in across:
            copy.wait_send()
        if ups:
            @pl.when(has_hi)
            def _():
                for copy in ups:
                    copy.wait_send()

            @pl.when(has_lo)
            def _():
                for copy in lows:
                    copy.wait_send()

    copies = [
        (
            [remote(send_hi, recv_lo, face_send.at[0], face_recv.at[0], upper_id)],
            [remote(send_lo, recv_hi, face_send.at[1], face_recv.at[1], lower_id)],
            [remote(send_z, recv_z, face_send.at[2], face_recv.at[2], other_id)],
        )
    ]
    exchange(*copies[0])

    for l in range(depth):
        share, rise = flow_fraction(wet[l])
        frac[l] = share
        slope[l] = rise
    carried = None
    for l in range(depth):
        up = (flags[l] & 4) != 0
        face = jnp.where(is_last_lane, 0.0, trans[2, l] * act[l] * next_y(act[l]))
        face_yu[l] = face
        face_yl[l] = prev_y(face)
        push, drive_here, drive_next = face_terms(
            face,
            (scaled[l], next_y(scaled[l])),
            (press[l], next_y(press[l])),
            (frac[l], next_y(frac[l])),
            (slope[l], next_y(slope[l])),
            up,
        )
        pushed = push - prev_y(push)
        driven = sat_res[l] + drive_here + prev_y(drive_next)
        if carried is not None:
            pushed = pushed - carried[0]
            driven = driven + carried[1]
        if l < depth - 1:
            face = trans[0, l] * act[l] * act[l + 1]
            face_z[l] = face
            push, drive_here, drive_next = face_terms(
                face,
                (scaled[l], scaled[l + 1]),
                (press[l], press[l + 1]),
                (frac[l], frac[l + 1]),
                (slope[l], slope[l + 1]),
                (flags[l] & 1) != 0,
            )
            pushed = pushed + push
            driven = driven + drive_here
            carried = (push, drive_next)
        resid[l] = pushed
        sat_res[l] = driven

    arrived(*copies[0])

    below = layer == 0
    z_share, z_rise = flow_fraction(recv_z[2])
    live = jnp.where(below, trans[0, edge] * edge_act * recv_z[3], recv_z[4] * edge_act)
    face_zedge[...] = live
    up_edge = jnp.where(below, send_z[5], recv_z[5]) > 0.5

    def ordered(mine, theirs):
        return jnp.where(below, mine, theirs), jnp.where(below, theirs, mine)

    push, drive_here, drive_next = face_terms(
        live,
        ordered(send_z[1], recv_z[1]),
        ordered(send_z[0], recv_z[0]),
        ordered(frac[edge], z_share),
        ordered(slope[edge], z_rise),
        up_edge,
    )
    resid[edge] = resid[edge] + jnp.where(below, push, -push)
    sat_res[edge] = sat_res[edge] + jnp.where(below, drive_here, drive_next)

    hi_share, hi_rise = flow_fraction(recv_hi[2])
    lo_share, lo_rise = flow_fraction(recv_lo[2])
    own_share, own_rise = flow_fraction(send_lo[2])
    low_face = recv_lo[3] * send_lo[3]
    low_push, _, low_drive = face_terms(
        low_face,
        (recv_lo[1], send_lo[1]),
        (recv_lo[0], send_lo[0]),
        (lo_share, own_share),
        (lo_rise, own_rise),
        recv_lo[4] > 0.5,
    )
    hi_press, hi_scaled, hi_act = recv_hi[0], recv_hi[1], recv_hi[3]

    def with_high(value, plane, l):
        return jnp.where(is_high_row, plane[l : l + 1], next_x(value))

    def with_low(value, plane, l):
        return jnp.where(is_low_row, plane[l : l + 1], prev_x(value))

    loads[8].wait()
    for l in range(depth):
        face = trans[1, l] * act[l] * with_high(act[l], hi_act, l)
        push, drive_here, drive_next = face_terms(
            face,
            (scaled[l], with_high(scaled[l], hi_scaled, l)),
            (press[l], with_high(press[l], hi_press, l)),
            (frac[l], with_high(frac[l], hi_share, l)),
            (slope[l], with_high(slope[l], hi_rise, l)),
            (flags[l] & 2) != 0,
        )
        resid[l] = resid[l] + push - with_low(push, low_push, l)
        sat_res[l] = sat_res[l] + drive_here + with_low(drive_next, low_drive, l)
        face_low = with_low(face, low_face, l)
        face_xu[l] = jnp.where(is_high_row, 0.0, face)
        face_xl[l] = jnp.where(is_low_row, 0.0, face_low)
        face_edge[l] = jnp.where(
            is_high_row, face, jnp.where(is_low_row, face_low, 0.0)
        )
        diagonal = comp[l] + face + face_low + face_yu[l] + face_yl[l]
        if l > 0:
            diagonal = diagonal + face_z[l - 1]
        else:
            diagonal = diagonal + jnp.where(below, 0.0, live)
        if l < depth - 1:
            diagonal = diagonal + face_z[l]
        else:
            diagonal = diagonal + jnp.where(below, live, 0.0)
        pivot = diagonal if l == 0 else diagonal - face_z[l - 1] * up_gain[l - 1]
        inverse = 1.0 / pivot
        inv_pivot[l] = inverse
        if l > 0:
            down_gain[l] = face_z[l - 1] * inverse
        if l < depth - 1:
            up_gain[l] = face_z[l] * inverse
        here = slice(l, l + 1)
        joint = face_z[l] if l < depth - 1 else live
        edge_face[here] = face[width - 1 : width]
        for k, plane in enumerate((face_low, face_yu[l], inverse, joint)):
            coef_hi[k, here] = plane[width - 1 : width]
        for k, plane in enumerate((face, face_yu[l], inverse, joint)):
            coef_lo[k, here] = plane[0:1]

    store_sat = pltpu.make_async_copy(sat_res, sat_out, out_sem.at[0])
    store_sat.start()

    def moment(left, right):
        total = None
        for l in range(depth):
            term = left[l] * right[l]
            total = term if total is None else total + term
        return total

    def fold(plane):
        total = plane[:, 0:128]
        for start in range(128, span, 128):
            total = total + plane[:, start : start + 128]
        return jnp.sum(total, axis=0, keepdims=True)

    halo_old = [None, None]

    def advance_halo(step):
            arrived(*late)
            if step == 0:
                arrived(*coefs)
            sides = (
                (got_lo, vec_lo, got_coef_lo, got_diag_lo, recv_lo[3] * send_lo[3]),
                (got_hi, vec_hi, got_coef_hi, got_diag_hi, edge_face[...]),
            )
            for side, (got, own, coef, diag, between) in enumerate(sides):
                beside_it = got[step, 0]
                value = (
                    coef[0] * got[step, 1]
                    + between * own[step, 0]
                    + coef[1] * next_y(beside_it)
                    + prev_y(coef[1] * beside_it)
                )
                joint = coef[3, depth - 1 : depth]
                value = value + jnp.where(strip_rows == edge, joint * diag[step], 0.0)
                if step > 0:
                    value = 2.0 * value - halo_old[side]
                halo_old[side] = value
                inverse = coef[2]
                scaled_value = value * inverse
                gain_up = coef[3] * inverse
                part = [scaled_value[0:1]]
                for l in range(1, depth):
                    gain = coef[3, l - 1 : l] * inverse[l : l + 1]
                    part.append(scaled_value[l : l + 1] + gain * part[l - 1])
                solved = part[depth - 1]
                got[step + 1, 0, depth - 1 : depth] = solved
                for l in range(depth - 2, -1, -1):
                    solved = part[l] + gain_up[l : l + 1] * solved
                    got[step + 1, 0, l : l + 1] = solved

    older = None
    current = [resid[l] for l in range(depth)]
    products = []
    for step in range(ITERS):
        partial = [current[0] * inv_pivot[0]]
        for l in range(1, depth):
            partial.append(current[l] * inv_pivot[l] + down_gain[l] * partial[l - 1])
        vector = [None] * depth
        vector[depth - 1] = partial[depth - 1]
        for l in range(depth - 2, -1, -1):
            vector[l] = partial[l] + up_gain[l] * vector[l + 1]
        wide = step % 2 == 0
        for l in range(depth):
            basis[step, l] = vector[l]
            if wide:
                here = slice(l, l + 1)
                vec_hi[step, 0, here] = vector[l][width - 1 : width]
                vec_hi[step, 1, here] = vector[l][width - 2 : width - 1]
                vec_lo[step, 0, here] = vector[l][0:1]
                vec_lo[step, 1, here] = vector[l][1:2]
        tag = 10 * step

        def hop(src, dst, target):
            nonlocal tag
            tag += 1
            return remote(src, dst, vec_send.at[tag - 1], vec_recv.at[tag - 1], target)

        ups, lows = [], []
        if wide:
            outer = basis[step, edge]
            diag_hi[step] = outer[width - 1 : width]
            diag_lo[step] = outer[0:1]
            ups = [
                hop(vec_hi.at[step, 0], got_lo.at[step, 0], upper_id),
            ]
            lows = [
                hop(vec_lo.at[step, 0], got_hi.at[step, 0], lower_id),
            ]
        trio = (ups, lows, [hop(basis.at[step, edge], got_z.at[step], other_id)])
        copies.append(trio)
        exchange(*trio)
        if wide:
            late = (
                [
                    hop(vec_hi.at[step, 1], got_lo.at[step, 1], upper_id),
                    hop(diag_hi.at[step], got_diag_lo.at[step], upper_diag),
                ],
                [
                    hop(vec_lo.at[step, 1], got_hi.at[step, 1], lower_id),
                    hop(diag_lo.at[step], got_diag_hi.at[step], lower_diag),
                ],
                [],
            )
            copies.append(late)
            exchange(*late)
        if step == 0:
            coefs = (
                [hop(coef_hi, got_coef_lo, upper_id)],
                [hop(coef_lo, got_coef_hi, lower_id)],
                [],
            )
            copies.append(coefs)
            exchange(*coefs)
        products.append(fold(moment(vector, current)))
        for l in range(depth):
            near = (
                face_xu[l] * next_x(vector[l])
                + face_xl[l] * prev_x(vector[l])
                + face_yu[l] * next_y(vector[l])
                + face_yl[l] * prev_y(vector[l])
            )
            source[l] = near
        arrived(*trio)
        if not wide:
            advance_halo(step - 1)
        source[edge] = source[edge] + face_zedge[...] * got_z[step]
        later = []
        for l in range(depth):
            halo = jnp.where(
                rows < width // 2, got_lo[step, 0, l : l + 1], got_hi[step, 0, l : l + 1]
            )
            value = source[l] + face_edge[l] * halo
            if step > 0:
                value = 2.0 * value - older[l]
            later.append(value)
        products.append(fold(moment(vector, later)))
        older, current = current, later

    for k, value in enumerate(products):
        sums[0, k : k + 1] = value
    sends = []
    slot = 0
    for place_of, stage in enumerate(stages):
        batch = [
            remote(
                sums.at[place_of], others.at[slot + k],
                sum_send.at[slot + k], sum_recv.at[slot + k], peer_id,
            )
            for k, peer_id in enumerate(stage)
        ]
        for copy in batch:
            copy.start()
        total = sums[place_of]
        for k, copy in enumerate(batch):
            copy.wait_recv()
        for k in range(len(batch)):
            total = total + others[slot + k]
        if place_of + 1 < len(stages):
            sums[place_of + 1] = total
        sends += batch
        slot += len(batch)
    total = jnp.sum(total, axis=1, keepdims=True)
    raw = [total[k : k + 1] for k in range(2 * ITERS)]
    moments = [raw[0], raw[1]]
    for k in range(2, 2 * ITERS):
        moments.append(2.0 * raw[k] - raw[k % 2])
    weights = [jnp.broadcast_to(value, (width, span)) for value in galerkin(moments)]
    for l in range(depth):
        value = weights[0] * basis[0, l]
        for step in range(1, ITERS):
            value = value + weights[step] * basis[step, l]
        sol_res[l] = value
    store_sol = pltpu.make_async_copy(sol_res, sol_out, out_sem.at[1])
    store_sol.start()
    for trio in copies:
        departed(*trio)
    for copy in sends:
        copy.wait_send()
    store_sat.wait()
    store_sol.wait()


def on_device(areal_count, *arrays):
    arrays = list(arrays)
    block = arrays[0].shape
    depth, width, span = block
    wells = arrays[7].shape[0]
    arrays[7] = arrays[7].reshape(1, wells)
    arrays[8] = arrays[8].reshape(1, wells)
    plane = (width, span)
    strip = (depth, span)
    low = min(LOW_GROUP, areal_count)
    slots = low + (areal_count // low - 1)
    f32 = jnp.float32
    cube = pltpu.VMEM(block, f32)

    def vmem(*shape):
        return pltpu.VMEM(shape, f32)

    scratch = [
        cube, cube, cube, cube, cube, vmem(3, *block), pltpu.VMEM(block, jnp.int32),
        pltpu.VMEM((1, wells), jnp.int32), vmem(1, wells),
        cube, cube, cube, cube, cube, cube,
        cube, cube, cube, cube,
        cube, cube, cube, cube, cube, vmem(*plane),
        vmem(ITERS, *block), cube,
        vmem(5, *strip), vmem(4, *strip), vmem(6, *plane),
        vmem(4, *strip), vmem(5, *strip), vmem(6, *plane),
        vmem(ITERS, 2, *strip), vmem(ITERS, 2, *strip),
        vmem(ITERS, 2, *strip), vmem(ITERS, 2, *strip), vmem(ITERS, *plane),
        vmem(4, *strip), vmem(4, *strip), vmem(4, *strip), vmem(4, *strip), vmem(*strip),
        vmem(ITERS, 1, span), vmem(ITERS, 1, span), vmem(ITERS, 1, span), vmem(ITERS, 1, span),
        vmem(3, 2 * ITERS, 128), vmem(slots, 2 * ITERS, 128),
        pltpu.SemaphoreType.DMA((9,)), pltpu.SemaphoreType.DMA((2,)),
        pltpu.SemaphoreType.DMA((3,)), pltpu.SemaphoreType.DMA((3,)),
        pltpu.SemaphoreType.DMA((10 * ITERS,)), pltpu.SemaphoreType.DMA((10 * ITERS,)),
        pltpu.SemaphoreType.DMA((slots,)), pltpu.SemaphoreType.DMA((slots,)),
    ]
    return pl.pallas_call(
        functools.partial(kernel, areal_count),
        out_shape=(jax.ShapeDtypeStruct(block, f32), jax.ShapeDtypeStruct(block, f32)),
        in_specs=[pl.BlockSpec(memory_space=pl.ANY)] * len(arrays),
        out_specs=(pl.BlockSpec(memory_space=pl.ANY), pl.BlockSpec(memory_space=pl.ANY)),
        scratch_shapes=scratch,
        compiler_params=pltpu.CompilerParams(
            collective_id=0, has_side_effects=True, vmem_limit_bytes=60 * 1024 * 1024
        ),
    )(*arrays)


def solution(mesh):
    block = P(("members", "layer"), "areal", None)
    return jax.shard_map(
        functools.partial(on_device, mesh.shape["areal"]),
        mesh=mesh,
        in_specs=(
            block, block, block, block, block,
            P(None, ("members", "layer"), "areal", None),
            block, P("members"), P("members"),
        ),
        out_specs=(block, block),
        check_vma=False,
    )
```
